256 devices in a mesh: dom: 32 (over y, x, core), head: 8 (over z).
Axes of the slice: x: 4, y: 4, z: 8, core: 2. Of those that a mesh axis runs over, the one named last changes fastest.
Arguments:
- features: bfloat16 [32768, 1024], P(('dom', 'head')), may hold values from -6 to 6
- norm_gain: float32 [1024], replicated, may hold values from 0.1 to 1.9
- in_proj: bfloat16 [1024, 3072], replicated, may hold values from -2.5 to 2.5, as said below
- out_proj: bfloat16 [1024, 1024], replicated, may hold values from -0.375 to 0.375
- adjacency: int32 [256, 8], P('dom'), may hold values from 0 to 255, as said below
- counts: int32 [256], P('dom'), may hold values from 3 to 8, as said below
Outputs:
- updated: bfloat16 [32768, 1024], P(('dom', 'head'))
The draws below stay inside these ranges and needn't reach their ends.
Inputs may be any that keep to these rules, and one draw needn't show every extreme that they name: `in_proj`: columns h * 3 * 64 + c * 64 + e hold head h's query (c = 0), key (c = 1) and value (c = 2) component e. `adjacency`: row t holds 8 distinct tile numbers; entry 0 is t itself. With a partition being 8 consecutive tiles, every entry lies in t's partition or one of the two beside it; entry 1 lies in the partition before t's and entry 2 in the one after (in the first and last partition both lie in the only neighbouring one). Only the first counts[t] entries of row t of adjacency are used.
All inputs are finite; a program needn't handle non-finite values.
Results may differ from the reference program's by a relative error of at most 0.015.
The reference program's roundings to bfloat16 on the way count: a program that leaves them out, or rounds other values in their place, can miss the bound.
Values may be sent and summed in bfloat16 or wider, within the bound.
No kernel may reach another device: no remote copies, remote signals or barrier semaphores. Data moves between devices by JAX's collectives and lax.ppermute only.
A program may use at most 128 MiB of HBM per device.

```python
import jax
import jax.numpy as jnp
from jax import lax

D = 1024
HEADS = 16
HEAD_DIM = 64
TILE = 128
NB = 8
GROUP_TILES = 8
TILES = 256
NODES = 32768
N_DOM = 32


def draw_in_proj(key, part):
    key = jax.random.fold_in(key, 11)
    normal_part = jax.random.truncated_normal(key, -6.0, 6.0, (D, HEADS * 3 * HEAD_DIM), jnp.float32) * D ** (-0.5)
    column = jnp.arange(HEADS * 3 * HEAD_DIM)
    component = column // HEAD_DIM % 3
    head_of = column // (3 * HEAD_DIM)
    head_scale = jnp.full((HEADS,), 1.5, jnp.float32)
    factor = jnp.where(component < 2, head_scale[head_of], 1.0)
    return jnp.clip(normal_part * factor, -2.5, 2.5).astype(jnp.bfloat16)


def draw_adjacency(key, part):
    key = jax.random.fold_in(key, 23)
    key_prev, key_next, key_rest = jax.random.split(key, 3)
    tile_ids = jnp.arange(TILES, dtype=jnp.int32)[:, None]
    group_of = tile_ids // GROUP_TILES
    prev_exists = group_of > 0
    next_exists = group_of < N_DOM - 1
    offset_one = jax.random.randint(key_prev, (TILES, 1), 0, GROUP_TILES)
    offset_two = (offset_one + 1 + jax.random.randint(key_next, (TILES, 1), 0, GROUP_TILES - 1)) % GROUP_TILES
    first_pick = jnp.where(prev_exists, (group_of - 1) * GROUP_TILES + offset_one, (group_of + 1) * GROUP_TILES + offset_one)
    second_pick = jnp.where(next_exists, (group_of + 1) * GROUP_TILES + offset_two, (group_of - 1) * GROUP_TILES + offset_two)
    window_pos = jnp.arange(3 * GROUP_TILES, dtype=jnp.int32)[None, :]
    candidate = (group_of - 1) * GROUP_TILES + window_pos
    usable = (candidate >= 0) & (candidate < TILES) & (candidate != tile_ids) & (candidate != first_pick) & (candidate != second_pick)
    scores = jax.random.randint(key_rest, (TILES, 3 * GROUP_TILES), 0, 65536) * (3 * GROUP_TILES) + window_pos
    scores = jnp.where(usable, scores, -1)
    chosen_pos = lax.top_k(scores, NB - 3)[1]
    chosen = (group_of - 1) * GROUP_TILES + chosen_pos
    return jnp.concatenate([tile_ids, first_pick, second_pick, chosen], axis=1).astype(jnp.int32)


def draw_counts(key, part):
    key = jax.random.fold_in(key, 37)
    sampled = jax.random.randint(key, (TILES,), 3, NB + 1)
    return sampled.at[0].set(NB).astype(jnp.int32)


def shard_levels(stream_key, extent, shards, low, top_value):
    loudness, own = 1.0, jax.random.fold_in(stream_key, 6)
    for axis_at, blocks in shards:
        steps = jnp.exp(jax.random.uniform(jax.random.fold_in(own, axis_at), (blocks,), jnp.float32, low / len(shards), top_value / len(shards)))
        loudness = loudness * jnp.repeat(steps, extent[axis_at] // blocks).reshape([-1 if axis == axis_at else 1 for axis in range(len(extent))])
    return loudness


def centred(stream_key, dims, scale, bound, cuts=(), held_as=jnp.bfloat16):
    result = jax.random.normal(stream_key, dims, jnp.float32) * scale
    if len(cuts) > 0:
        result = shard_levels(stream_key, dims, cuts, -0.22, 0.18) * result
    return jnp.clip(result, min=-bound, max=bound).astype(held_as)


def setup_inputs(seed: int = 0) -> dict:
    key_list = jax.random.split(jax.random.key(seed), 7)
    features = centred(key_list[0], (NODES, D), 1.0, 6.0, ((0, 256),))
    norm_gain = jnp.clip(1.0 + 0.18 * jax.random.normal(key_list[1], (D,), jnp.float32), 0.1, 1.9)
    in_proj = draw_in_proj(jax.random.fold_in(key_list[6], 71), 0)
    out_proj = centred(key_list[3], (D, D), (D // 4) ** -0.5, 0.375)
    adjacency = draw_adjacency(jax.random.fold_in(key_list[6], 71), 0)
    counts = draw_counts(jax.random.fold_in(key_list[6], 71), 0)
    return dict(features=features, norm_gain=norm_gain, in_proj=in_proj, out_proj=out_proj, adjacency=adjacency, counts=counts)


epsilon = 1e-05

def rms_normed(features, norm_gain):
    widened = features.astype(jnp.float32)
    power = lax.optimization_barrier(jnp.mean(widened * widened, axis=-1, keepdims=True))
    return (widened, (widened * lax.rsqrt(power + epsilon) * norm_gain).astype(jnp.bfloat16))

def reference(features, norm_gain, in_proj, out_proj, adjacency, counts):
    widened, normed = rms_normed(features, norm_gain)
    stacked = lax.optimization_barrier(jnp.dot(normed, in_proj, preferred_element_type=jnp.float32).astype(jnp.bfloat16))
    layout = stacked.astype(jnp.float32).reshape(TILES, TILE, HEADS, 3, HEAD_DIM)
    queries = layout[:, :, :, 0]
    key_value = layout[:, :, :, 1:]
    slot_tile = jnp.arange(NB * TILE) // TILE

    def one_tile(pieces):
        query_tile, tile_list, count = pieces
        picked = key_value[tile_list]
        keys = picked[:, :, :, 0].reshape(NB * TILE, HEADS, HEAD_DIM)
        values = picked[:, :, :, 1].reshape(NB * TILE, HEADS, HEAD_DIM)
        scores = jnp.einsum('qhd,khd->hqk', query_tile, keys) * HEAD_DIM ** (-0.5)
        scores = jnp.where((slot_tile < count)[None, None, :], scores, -1e+30)
        row_max = lax.optimization_barrier(jnp.max(scores, axis=-1, keepdims=True))
        powers = jnp.exp(scores - row_max)
        totals = lax.optimization_barrier(jnp.sum(powers, axis=-1, keepdims=True))
        weights = lax.optimization_barrier((powers / totals).astype(jnp.bfloat16)).astype(jnp.float32)
        mixed = jnp.einsum('hqk,khd->qhd', weights, values)
        return mixed.reshape(TILE, HEADS * HEAD_DIM).astype(jnp.bfloat16)
    attended = lax.map(one_tile, (queries, adjacency, counts)).reshape(NODES, D)
    return (widened + jnp.dot(attended, out_proj, preferred_element_type=jnp.float32)).astype(jnp.bfloat16)
```

```python
import functools

import jax
import jax.numpy as jnp
from jax import lax
from jax.experimental import pallas as pl
from jax.experimental.pallas import tpu as pltpu
from jax.sharding import PartitionSpec as P

HEADS = 16
HEAD_DIM = 64
TILE = 128
NB = 8
D = 1024
PAIRS = HEADS // 2
STATS = 3 * HEADS
LOW = -1e30
epsilon = 1e-05
VMEM = pl.BlockSpec(memory_space=pltpu.VMEM)
SMEM = pl.BlockSpec(memory_space=pltpu.SMEM)
PARAMS = pltpu.CompilerParams(vmem_limit_bytes=40 * 1024 * 1024)


def normed(features, gain):
    wide = features.astype(jnp.float32)
    power = jnp.mean(wide * wide, axis=-1, keepdims=True)
    return (wide * lax.rsqrt(power + epsilon) * gain).astype(jnp.bfloat16)


def sort_kernel(w_ref, q_ref, kv_ref):
    low = lax.broadcasted_iota(jnp.int32, (w_ref.shape[0], 128), 1) < HEAD_DIM
    for j in range(PAIRS):
        t0, t1, t2 = (w_ref[:, pl.ds(j * 384 + c * 128, 128)] for c in range(3))
        at = pl.ds(j * 128, 128)
        q_ref[:, at] = jnp.where(low, t0, t1)
        kv_ref[:, at] = jnp.where(low, t2, t0)
        kv_ref[:, pl.ds(D + j * 128, 128)] = jnp.where(low, t1, t2)


def sort_weights(in_proj):
    rows = 128
    return pl.pallas_call(
        sort_kernel,
        grid=(D // rows,),
        in_specs=[pl.BlockSpec((rows, 3 * D), lambda i: (i, 0))],
        out_specs=[
            pl.BlockSpec((rows, D), lambda i: (i, 0)),
            pl.BlockSpec((rows, 2 * D), lambda i: (i, 0)),
        ],
        out_shape=[
            jax.ShapeDtypeStruct((D, D), jnp.bfloat16),
            jax.ShapeDtypeStruct((D, 2 * D), jnp.bfloat16),
        ],
        compiler_params=PARAMS,
        cost_estimate=pl.CostEstimate(flops=0, bytes_accessed=12 * 1024 * 1024, transcendentals=0),
        name="sort_weights",
    )(in_proj)


def query_kernel(count, *refs):
    features, gain_ref, w_ref, q_ref = refs[:count], *refs[count:]
    for n in range(count):
        rows = normed(features[n][:TILE], gain_ref[...])
        for c in range(2):
            part = jnp.dot(rows, w_ref[:, pl.ds(c * 512, 512)], preferred_element_type=jnp.float32)
            part = part.astype(jnp.bfloat16).astype(jnp.float32) * HEAD_DIM ** (-0.5)
            for j in range(4):
                turned = pltpu.roll(part[:, j * 128 : (j + 1) * 128], HEAD_DIM, 1)
                q_ref[n, :, pl.ds(c * 512 + j * 128, 128)] = turned.astype(jnp.bfloat16)


def project_queries(arrays, gain, w_query):
    count = len(arrays)
    return pl.pallas_call(
        functools.partial(query_kernel, count),
        in_specs=[VMEM] * (count + 2),
        out_specs=VMEM,
        out_shape=jax.ShapeDtypeStruct((count, TILE, D), jnp.bfloat16),
        compiler_params=PARAMS,
        cost_estimate=pl.CostEstimate(
            flops=2 * count * TILE * D * D, bytes_accessed=4 * 1024 * 1024, transcendentals=0
        ),
        name="project_queries",
    )(*arrays, gain, w_query)


def kv_kernel(count, *refs):
    features, (gain_ref, w_ref, k_ref, vt_ref, rows_ref) = refs[:count], refs[count:]
    step = pl.program_id(0)

    @pl.when(step == 0)
    def _():
        at = 0
        for ref in features:
            rows_ref[at : at + ref.shape[0]] = normed(ref[...], gain_ref[...])
            at += ref.shape[0]

    part = jnp.dot(rows_ref[...], w_ref[...], preferred_element_type=jnp.float32)

    @pl.when(step < 2)
    def _():
        k_ref[...] = part.astype(jnp.bfloat16)

    @pl.when(step >= 2)
    def _():
        vt_ref[...] = part.T.astype(jnp.bfloat16)


def project_kv(arrays, gain, w_kv):
    total = sum(a.shape[0] for a in arrays)
    return pl.pallas_call(
        functools.partial(kv_kernel, len(arrays)),
        grid=(4,),
        in_specs=[pl.BlockSpec(a.shape, lambda i: (0, 0)) for a in arrays]
        + [
            pl.BlockSpec((1, D), lambda i: (0, 0)),
            pl.BlockSpec((D, 512), lambda i: (0, i)),
        ],
        out_specs=[
            pl.BlockSpec((total, 512), lambda i: (0, jnp.minimum(i, 1))),
            pl.BlockSpec((512, total), lambda i: (jnp.maximum(i - 2, 0), 0)),
        ],
        out_shape=[
            jax.ShapeDtypeStruct((total, D), jnp.bfloat16),
            jax.ShapeDtypeStruct((D, total), jnp.bfloat16),
        ],
        scratch_shapes=[pltpu.VMEM((total, D), jnp.bfloat16)],
        compiler_params=PARAMS,
        cost_estimate=pl.CostEstimate(
            flops=4 * total * D * D, bytes_accessed=5 * 1024 * 1024, transcendentals=0
        ),
        name="project_kv",
    )(*arrays, gain, w_kv)


def attend_tile(n, q_ref, k_ref, vt_ref, at, m_ref, l_ref, acc_ref):
    low = lax.broadcasted_iota(jnp.int32, (TILE, 128), 1) < HEAD_DIM
    for j in range(PAIRS):
        cols = pl.ds(j * 128, 128)
        query = q_ref[n, :, cols]
        zero = jnp.zeros_like(query)
        both = jnp.concatenate([jnp.where(low, query, zero), jnp.where(low, zero, query)], axis=0)
        scores = lax.dot_general(
            k_ref[at : at + TILE, cols], both, (((1,), (1,)), ((), ())), preferred_element_type=jnp.float32
        )
        old = m_ref[n, j : j + 1]
        new = jnp.maximum(old, jnp.max(scores, axis=0, keepdims=True))
        powers = jnp.exp(scores - new)
        fade = jnp.exp(old - new)
        m_ref[n, j : j + 1] = new
        l_ref[n, j : j + 1] = l_ref[n, j : j + 1] * fade + jnp.sum(powers, axis=0, keepdims=True)
        mixed = jnp.dot(
            vt_ref[cols, at : at + TILE], powers.astype(jnp.bfloat16), preferred_element_type=jnp.float32
        )
        even, odd = pl.ds(j * 128, HEAD_DIM), pl.ds(j * 128 + HEAD_DIM, HEAD_DIM)
        acc_ref[n, even] = acc_ref[n, even] * fade[:, TILE:] + mixed[:HEAD_DIM, TILE:]
        acc_ref[n, odd] = acc_ref[n, odd] * fade[:, :TILE] + mixed[HEAD_DIM:, :TILE]


def attend_kernel(steps, *refs):
    flags_ref, q_own, q_near = refs[:3]
    keys = refs[3 : 3 + 2 * len(steps)]
    own_ref, stats_ref, core_ref, cross_ref, m_ref, l_ref, acc_ref = refs[3 + 2 * len(steps) :]
    m_ref[...] = jnp.full_like(m_ref, LOW)
    l_ref[...] = jnp.zeros_like(l_ref)
    acc_ref[...] = jnp.zeros_like(acc_ref)
    here = flags_ref[24]
    for n in range(3):
        q_ref, row = (q_own, 0) if n == 0 else (q_near, n - 1)
        for s, shifts in enumerate(steps):
            k_ref, vt_ref = keys[2 * s], keys[2 * s + 1]
            for place, shift in enumerate(shifts):
                tile = lax.rem(here + (shift + 8), 8)

                @pl.when(flags_ref[n * 8 + tile] != 0)
                def _():
                    attend_tile(
                        row,
                        q_ref,
                        k_ref,
                        vt_ref,
                        place * TILE,
                        m_ref.at[pl.ds(n - row, 2)],
                        l_ref.at[pl.ds(n - row, 2)],
                        acc_ref.at[pl.ds(n - row, 2)],
                    )

    own_ref[...] = acc_ref[0]
    stats_ref[0] = m_ref[0]
    stats_ref[1] = l_ref[0]
    for n, out_ref in ((1, core_ref), (2, cross_ref)):
        total = l_ref[n]
        some = total > 0
        safe = jnp.where(some, total, 1.0)
        inverse = 1.0 / safe
        lse = jnp.where(some, m_ref[n] + jnp.log(safe), LOW)
        for j in range(PAIRS):
            even, odd = pl.ds(j * 128, HEAD_DIM), pl.ds(j * 128 + HEAD_DIM, HEAD_DIM)
            out_ref[even] = (acc_ref[n, even] * inverse[j : j + 1, TILE:]).astype(jnp.bfloat16)
            out_ref[odd] = (acc_ref[n, odd] * inverse[j : j + 1, :TILE]).astype(jnp.bfloat16)
        stacked = jnp.concatenate([lse[:, :TILE], lse[:, TILE:]], axis=0)
        for c in range(3):
            term = stacked.astype(jnp.bfloat16)
            out_ref[pl.ds(D + c * HEADS, HEADS)] = term
            stacked = stacked - term.astype(jnp.float32)


def attend(flags, q_own, q_near, kv):
    steps = [shifts for shifts, _, _ in kv]
    arrays = [a for _, k, vt in kv for a in (k, vt)]
    partial = jax.ShapeDtypeStruct((D + STATS, TILE), jnp.bfloat16)
    return pl.pallas_call(
        functools.partial(attend_kernel, steps),
        in_specs=[SMEM] + [VMEM] * (2 + len(arrays)),
        out_specs=[VMEM] * 4,
        out_shape=[
            jax.ShapeDtypeStruct((D, TILE), jnp.float32),
            jax.ShapeDtypeStruct((2, PAIRS, 2 * TILE), jnp.float32),
            partial,
            partial,
        ],
        scratch_shapes=[
            pltpu.VMEM((3, PAIRS, 2 * TILE), jnp.float32),
            pltpu.VMEM((3, PAIRS, 2 * TILE), jnp.float32),
            pltpu.VMEM((3, D, TILE), jnp.float32),
        ],
        compiler_params=PARAMS,
        cost_estimate=pl.CostEstimate(
            flops=10 * 8 * TILE * TILE * D, bytes_accessed=6 * 1024 * 1024, transcendentals=0
        ),
        name="attend",
    )(flags, q_own, q_near, *arrays)


def finish_kernel(near_ref, own_ref, stats_ref, core_ref, cross_ref, w_ref, features_ref, out_ref, sum_ref):
    def split(x):
        return jnp.concatenate([x[:, :TILE], x[:, TILE:]], axis=0)

    def received(ref, usable):
        terms = [ref[pl.ds(D + c * HEADS, HEADS)].astype(jnp.float32) for c in range(3)]
        return jnp.where(usable, terms[0] + terms[1] + terms[2], LOW)

    total = split(stats_ref[1])
    lse = [
        split(stats_ref[0]) + jnp.log(total),
        received(core_ref, near_ref[0] != 0),
        received(cross_ref, near_ref[1] != 0),
    ]
    top = jnp.maximum(jnp.maximum(lse[0], lse[1]), lse[2])
    parts = [jnp.exp(x - top) for x in lse]
    inverse = 1.0 / (parts[0] + parts[1] + parts[2])
    scale = [parts[0] * inverse / total, parts[1] * inverse, parts[2] * inverse]
    for h in range(HEADS):
        row = h // 2 + (PAIRS if h % 2 == 0 else 0)
        at = pl.ds(h * HEAD_DIM, HEAD_DIM)
        mixed = own_ref[at] * scale[0][row : row + 1]
        mixed += core_ref[at].astype(jnp.float32) * scale[1][row : row + 1]
        mixed += cross_ref[at].astype(jnp.float32) * scale[2][row : row + 1]
        sum_ref[at] = mixed
    attended = sum_ref[...].T.astype(jnp.bfloat16)
    for c in range(2):
        at = pl.ds(c * 512, 512)
        product = jnp.dot(attended, w_ref[:, at], preferred_element_type=jnp.float32)
        out_ref[:, at] = (features_ref[:, at].astype(jnp.float32) + product).astype(jnp.bfloat16)


def finish(near, own, stats, core, cross, out_proj, features):
    return pl.pallas_call(
        finish_kernel,
        in_specs=[SMEM] + [VMEM] * 6,
        out_specs=VMEM,
        out_shape=jax.ShapeDtypeStruct((TILE, D), jnp.bfloat16),
        scratch_shapes=[pltpu.VMEM((D, TILE), jnp.float32)],
        compiler_params=PARAMS,
        cost_estimate=pl.CostEstimate(
            flops=2 * TILE * D * D, bytes_accessed=4 * 1024 * 1024, transcendentals=0
        ),
        name="finish",
    )(near, own, stats, core, cross, out_proj, features)


def body(features, norm_gain, in_proj, out_proj, adjacency, counts):
    here, group = lax.axis_index("head"), lax.axis_index("dom")
    group_count, around = lax.axis_size("dom"), lax.axis_size("head")
    gain = norm_gain.reshape(1, D)

    up = [(i, (i + 1) % around) for i in range(around)]
    down = [(j, i) for i, j in up]
    swap = [(i, i ^ 1) for i in range(group_count)]
    hop = [(i, i + 1) for i in range(1, group_count - 1, 2)]
    hop = hop + [(j, i) for i, j in hop]

    row = lax.dynamic_slice_in_dim(adjacency, here, 1, 0)[0]
    used = jnp.arange(NB) < lax.dynamic_slice_in_dim(counts, here, 1, 0)[0]

    def needed(partition):
        tiles = partition * NB + jnp.arange(NB)
        return jnp.any((row[None, :] == tiles[:, None]) & used[None, :], axis=1)

    core_group = group ^ 1
    cross_group = jnp.where(group % 2 == 1, group + 1, group - 1)
    need_own, need_core, need_cross = needed(group), needed(core_group), needed(cross_group)
    near = jnp.stack([jnp.any(need_core), jnp.any(need_cross)]).astype(jnp.int32)
    wanted = jnp.concatenate([need_core, need_cross]).astype(jnp.bfloat16)
    parcel = jnp.concatenate([features, jnp.pad(wanted[None], ((0, 15), (0, D - 16)))], axis=0)

    forward, backward = lax.ppermute(features, "head", up), lax.ppermute(features, "head", down)
    from_core = lax.ppermute(parcel, "dom", swap)
    from_cross = lax.ppermute(parcel, "dom", hop)
    flags = jnp.concatenate(
        [
            need_own.astype(jnp.int32),
            from_core[TILE, :8].astype(jnp.int32),
            from_cross[TILE, 8:16].astype(jnp.int32),
            here[None].astype(jnp.int32),
        ]
    )

    w_query, w_kv = sort_weights(in_proj)
    q_own = project_queries([features], gain, w_query)
    kv = [((0,), *project_kv([features], gain, w_kv))]
    q_near = project_queries([from_core, from_cross], gain, w_query)
    for step in range(1, 4):
        arrived = [forward, backward]
        if step < 3:
            forward, backward = (
                lax.ppermute(forward, "head", up),
                lax.ppermute(backward, "head", down),
            )
        else:
            half = TILE // 2
            last = [
                lax.ppermute(forward[:half], "head", up),
                lax.ppermute(backward[half:], "head", down),
            ]
        kv.append(((-step, step), *project_kv(arrived, gain, w_kv)))
    kv.append(((4,), *project_kv(last, gain, w_kv)))

    own, stats, to_core, to_cross = attend(flags, q_own, q_near, kv)
    core = lax.ppermute(to_core, "dom", swap)
    cross = lax.ppermute(to_cross, "dom", hop)
    return finish(near, own, stats, core, cross, out_proj, features)


def solution(mesh):
    return jax.shard_map(
        body,
        mesh=mesh,
        in_specs=(P(("dom", "head"), None), P(), P(), P(), P("dom", None), P("dom")),
        out_specs=P(("dom", "head"), None),
        check_vma=False,
    )
```

```python
import functools

import jax
import jax.numpy as jnp
from jax import lax
from jax.experimental import pallas as pl
from jax.experimental.pallas import tpu as pltpu
from jax.sharding import PartitionSpec as P

HEADS = 16
HEAD_DIM = 64
TILE = 128
NB = 8
D = 1024
PAIRS = HEADS // 2
STATS = 4 * HEADS
PARTS = 8
LOW = -1e30
epsilon = 1e-05
VMEM = pl.BlockSpec(memory_space=pltpu.VMEM)
SMEM = pl.BlockSpec(memory_space=pltpu.SMEM)
PARAMS = pltpu.CompilerParams(vmem_limit_bytes=40 * 1024 * 1024)


def normed(features, gain):
    wide = features.astype(jnp.float32)
    power = jnp.mean(wide * wide, axis=-1, keepdims=True)
    return (wide * lax.rsqrt(power + epsilon) * gain).astype(jnp.bfloat16)


def prepare_kernel(
    features_ref, adjacency_ref, counts_ref, w_ref, parcel_ref, q_ref, kv_ref, lists_ref, amounts_ref, held_ref, sems
):
    rows = D // PARTS
    copies = [
        pltpu.make_async_copy(features_ref, parcel_ref.at[pl.ds(0, TILE)], sems.at[0]),
        pltpu.make_async_copy(adjacency_ref, lists_ref, sems.at[1]),
        pltpu.make_async_copy(counts_ref, amounts_ref, sems.at[2]),
    ]
    for i in range(PARTS):
        at = pl.ds(i * rows, rows)
        copies.append(pltpu.make_async_copy(w_ref.at[at], held_ref.at[at], sems.at[3 + i]))
    for copy in copies:
        copy.start()
    for copy in copies[:3]:
        copy.wait()
    lists = jnp.concatenate([lists_ref[...], amounts_ref[...], jnp.zeros((7, NB), jnp.int32)], axis=0)
    parcel_ref[pl.ds(TILE, 16)] = jnp.zeros((16, D), jnp.bfloat16)
    parcel_ref[pl.ds(TILE, 16), :NB] = lists.astype(jnp.float32).astype(jnp.bfloat16)
    low = lax.broadcasted_iota(jnp.int32, (rows, 128), 1) < HEAD_DIM
    for i, copy in enumerate(copies[3:]):
        copy.wait()
        at = pl.ds(i * rows, rows)
        for j in range(PAIRS):
            t0, t1, t2 = (held_ref[at, pl.ds(j * 384 + c * 128, 128)] for c in range(3))
            q_ref[at, pl.ds(j * 128, 128)] = jnp.where(low, t0, t1)
            kv_ref[at, pl.ds(j * 128, 128)] = jnp.where(low, t2, t0)
            kv_ref[at, pl.ds(D + j * 128, 128)] = jnp.where(low, t1, t2)


def prepare(features, adjacency, counts, in_proj):
    arrays = (features, adjacency, counts, in_proj)
    return pl.pallas_call(
        prepare_kernel,
        in_specs=[pl.BlockSpec(memory_space=pltpu.HBM)] * 4,
        out_specs=[VMEM] * 3,
        out_shape=[
            jax.ShapeDtypeStruct((TILE + 16, D), jnp.bfloat16),
            jax.ShapeDtypeStruct((D, D), jnp.bfloat16),
            jax.ShapeDtypeStruct((D, 2 * D), jnp.bfloat16),
        ],
        scratch_shapes=[
            pltpu.VMEM((NB, NB), jnp.int32),
            pltpu.VMEM((1, NB), jnp.int32),
            pltpu.VMEM((D, 3 * D), jnp.bfloat16),
            pltpu.SemaphoreType.DMA((3 + PARTS,)),
        ],
        compiler_params=PARAMS,
        cost_estimate=pl.CostEstimate(flops=0, bytes_accessed=12 * 1024 * 1024, transcendentals=0),
        name="prepare",
    )(*(pltpu.with_memory_space_constraint(a, pltpu.HBM) for a in arrays))


def project_queries(rows, w_ref, q_ref, n):
    for c in range(2):
        part = jnp.dot(rows, w_ref[:, c * 512 : (c + 1) * 512], preferred_element_type=jnp.float32)
        part = part.astype(jnp.bfloat16).astype(jnp.float32) * HEAD_DIM ** (-0.5)
        for j in range(4):
            turned = pltpu.roll(part[:, j * 128 : (j + 1) * 128], HEAD_DIM, 1)
            q_ref[n, :, c * 512 + j * 128 : c * 512 + (j + 1) * 128] = turned.astype(jnp.bfloat16)


def near_kernel(core_ref, cross_ref, parcel_ref, gain_ref, w_ref, q_ref, info_ref):
    here, group = lax.axis_index("head"), lax.axis_index("dom")
    row = lax.broadcasted_iota(jnp.int32, (16, 128), 0)
    lane = lax.broadcasted_iota(jnp.int32, (16, 128), 1)
    info = jnp.zeros((1, 1), jnp.float32)
    for n, ref in enumerate((parcel_ref, core_ref, cross_ref)):
        if n > 0:
            project_queries(normed(ref[:TILE], gain_ref[...]), w_ref, q_ref, n - 1)
        lists = ref[pl.ds(TILE, 16), :128].astype(jnp.float32).astype(jnp.int32)
        count = jnp.where((row == NB) & (lane == here), lists, 0).astype(jnp.float32)
        count = jnp.sum(jnp.sum(count, axis=0, keepdims=True), axis=1, keepdims=True)
        used = (row == here) & (lane < jnp.minimum(count, NB).astype(jnp.int32))
        used = used & (jnp.right_shift(lists, 3) == group)
        bits = jnp.where(used, jnp.left_shift(1, (lists & (NB - 1)) + n * NB), 0).astype(jnp.float32)
        info = info + jnp.sum(jnp.sum(bits, axis=0, keepdims=True), axis=1, keepdims=True)
    info_ref[...] = jnp.broadcast_to(info, info_ref.shape)


def project_near(core, cross, parcel, gain, w_query):
    return pl.pallas_call(
        near_kernel,
        in_specs=[VMEM] * 5,
        out_specs=[VMEM] * 2,
        out_shape=[
            jax.ShapeDtypeStruct((2, TILE, D), jnp.bfloat16),
            jax.ShapeDtypeStruct((8, 128), jnp.float32),
        ],
        compiler_params=PARAMS,
        cost_estimate=pl.CostEstimate(
            flops=4 * TILE * D * D, bytes_accessed=4 * 1024 * 1024, transcendentals=0
        ),
        name="project_near",
    )(core, cross, parcel, gain, w_query)


def project_kernel(count, with_query, *refs):
    features, gain_ref, refs = refs[:count], refs[count], refs[count + 1 :]
    if with_query:
        wq_ref, w_ref, q_ref, k_ref, vt_ref, rows_ref = refs
    else:
        w_ref, k_ref, vt_ref, rows_ref = refs
    at = 0
    for ref in features:
        rows_ref[at : at + ref.shape[0]] = normed(ref[...], gain_ref[...])
        at += ref.shape[0]
    if with_query:
        project_queries(rows_ref[:TILE], wq_ref, q_ref, 0)
    for c in range(2):
        at = slice(c * 512, (c + 1) * 512)
        part = jnp.dot(rows_ref[...], w_ref[:, at], preferred_element_type=jnp.float32)
        k_ref[:, at] = part.astype(jnp.bfloat16)
    for c in range(2):
        at, cols = slice(c * 512, (c + 1) * 512), slice(D + c * 512, D + (c + 1) * 512)
        part = jnp.dot(rows_ref[...], w_ref[:, cols], preferred_element_type=jnp.float32)
        vt_ref[at] = part.T.astype(jnp.bfloat16)


def project(arrays, gain, w_kv, w_query=None):
    total, query = sum(a.shape[0] for a in arrays), w_query is not None
    return pl.pallas_call(
        functools.partial(project_kernel, len(arrays), query),
        in_specs=[VMEM] * (len(arrays) + 2 + query),
        out_specs=[VMEM] * (2 + query),
        out_shape=[jax.ShapeDtypeStruct((1, TILE, D), jnp.bfloat16)] * query
        + [
            jax.ShapeDtypeStruct((total, D), jnp.bfloat16),
            jax.ShapeDtypeStruct((D, total), jnp.bfloat16),
        ],
        scratch_shapes=[pltpu.VMEM((total, D), jnp.bfloat16)],
        compiler_params=PARAMS,
        cost_estimate=pl.CostEstimate(
            flops=4 * total * D * D, bytes_accessed=5 * 1024 * 1024, transcendentals=0
        ),
        name="project",
    )(*arrays, gain, *([w_query] * query), w_kv)


def attend_tile(q_ref, k_ref, vt_ref, at, m_ref, l_ref, acc_ref):
    low = lax.broadcasted_iota(jnp.int32, (TILE, 128), 1) < HEAD_DIM
    old, total = m_ref[...], l_ref[...]
    scores, powers, tops, sums = [], [], [], []
    for j in range(PAIRS):
        cols = slice(j * 128, (j + 1) * 128)
        query = q_ref[:, cols]
        zero = jnp.zeros_like(query)
        both = jnp.concatenate([jnp.where(low, query, zero), jnp.where(low, zero, query)], axis=0)
        scores.append(
            lax.dot_general(
                k_ref[at : at + TILE, cols],
                both,
                (((1,), (1,)), ((), ())),
                preferred_element_type=jnp.float32,
            )
        )
    for j in range(PAIRS):
        top = jnp.maximum(old[j : j + 1], jnp.max(scores[j], axis=0, keepdims=True))
        power = jnp.exp(scores[j] - top)
        tops.append(top)
        sums.append(jnp.sum(power, axis=0, keepdims=True))
        powers.append(power.astype(jnp.bfloat16))
    new = jnp.concatenate(tops, axis=0)
    fade = jnp.exp(old - new)
    m_ref[...] = new
    l_ref[...] = total * fade + jnp.concatenate(sums, axis=0)
    for j in range(PAIRS):
        for half, lanes in ((0, slice(TILE, 2 * TILE)), (1, slice(0, TILE))):
            rows = slice(j * 128 + half * HEAD_DIM, j * 128 + (half + 1) * HEAD_DIM)
            mixed = jnp.dot(
                vt_ref[rows, at : at + TILE], powers[j][:, lanes], preferred_element_type=jnp.float32
            )
            acc_ref[rows] = acc_ref[rows] * fade[j : j + 1, lanes] + mixed


def attend_kernel(who, steps, first, last, *refs):
    info_ref, q_refs, refs = refs[0], refs[1 : 1 + len(who)], refs[1 + len(who) :]
    keys, refs = refs[: 2 * len(steps)], refs[2 * len(steps) :]
    if not first:
        refs = refs[3:]
    m_ref, l_ref, acc_ref = refs[:3]
    if first:
        m_ref[...] = jnp.full_like(m_ref, LOW)
        l_ref[...] = jnp.zeros_like(l_ref)
        acc_ref[...] = jnp.zeros_like(acc_ref)
    here, turn = lax.axis_index("head"), 1 - 2 * (lax.axis_index("dom") % 2)
    info = jnp.max(info_ref[...]).astype(jnp.int32)
    for n, (q_ref, (flag, row)) in enumerate(zip(q_refs, who)):
        for s, shifts in enumerate(steps):
            k_ref, vt_ref = keys[2 * s], keys[2 * s + 1]
            for place, shift in enumerate(shifts):
                tile = lax.rem(here + turn * shift + 8, 8)

                @pl.when(jnp.right_shift(info, flag * NB + tile) & 1 != 0)
                def _():
                    attend_tile(
                        q_ref.at[row], k_ref, vt_ref, place * TILE, m_ref.at[n], l_ref.at[n], acc_ref.at[n]
                    )

    if not last:
        return
    n, out_ref = len(who) - 1, refs[3]
    total = l_ref[n]
    some = total > 0
    safe = jnp.where(some, total, 1.0)
    inverse = 1.0 / safe
    lse = jnp.where(some, m_ref[n] + jnp.log(safe), LOW)
    for j in range(PAIRS):
        even, odd = pl.ds(j * 128, HEAD_DIM), pl.ds(j * 128 + HEAD_DIM, HEAD_DIM)
        out_ref[even] = (acc_ref[n, even] * inverse[j : j + 1, TILE:]).astype(jnp.bfloat16)
        out_ref[odd] = (acc_ref[n, odd] * inverse[j : j + 1, :TILE]).astype(jnp.bfloat16)
    stacked = jnp.concatenate([lse[:, :TILE], lse[:, TILE:]], axis=0)
    for c in range(3):
        term = stacked.astype(jnp.bfloat16)
        out_ref[pl.ds(D + c * HEADS, HEADS)] = term
        stacked = stacked - term.astype(jnp.float32)
    out_ref[pl.ds(D + 3 * HEADS, HEADS)] = jnp.ones((HEADS, TILE), jnp.bfloat16)


def attend(info, queries, kv, state=(), last=False):
    who, steps = [q[1:] for q in queries], [shifts for shifts, _, _ in kv]
    arrays = [q[0] for q in queries] + [a for _, k, vt in kv for a in (k, vt)]
    at = 1 + len(arrays)
    return pl.pallas_call(
        functools.partial(attend_kernel, who, steps, not state, last),
        in_specs=[VMEM] * (at + len(state)),
        out_specs=[VMEM] * (4 if last else 3),
        out_shape=[
            jax.ShapeDtypeStruct((len(who), PAIRS, 2 * TILE), jnp.float32),
            jax.ShapeDtypeStruct((len(who), PAIRS, 2 * TILE), jnp.float32),
            jax.ShapeDtypeStruct((len(who), D, TILE), jnp.float32),
        ]
        + [jax.ShapeDtypeStruct((D + STATS, TILE), jnp.bfloat16)] * last,
        input_output_aliases={at + i: i for i in range(len(state))},
        compiler_params=PARAMS,
        cost_estimate=pl.CostEstimate(
            flops=16 * TILE * TILE * D * len(kv), bytes_accessed=4 * 1024 * 1024, transcendentals=0
        ),
        name="attend",
    )(info, *arrays, *state)


def split(x):
    return jnp.concatenate([x[:, :TILE], x[:, TILE:]], axis=0)


def received(ref):
    terms = [ref[pl.ds(D + c * HEADS, HEADS)].astype(jnp.float32) for c in range(4)]
    return jnp.where(terms[3] > 0, terms[0] + terms[1] + terms[2], LOW)


def first_kernel(m_ref, l_ref, cross_ref, lse_ref):
    lse_ref[0] = split(m_ref[0]) + jnp.log(split(l_ref[0]))
    lse_ref[1] = received(cross_ref)


def finish_first(m, l, cross):
    return pl.pallas_call(
        first_kernel,
        in_specs=[VMEM] * 3,
        out_specs=VMEM,
        out_shape=jax.ShapeDtypeStruct((2, HEADS, TILE), jnp.float32),
        compiler_params=PARAMS,
        cost_estimate=pl.CostEstimate(flops=0, bytes_accessed=2 * 1024 * 1024, transcendentals=0),
        name="finish_first",
    )(m, l, cross)


def finish_kernel(lse_ref, l_ref, own_ref, core_ref, cross_ref, w_ref, features_ref, out_ref, sum_ref, made_ref, sems):
    total = split(l_ref[0])
    lse = [lse_ref[0], received(core_ref), lse_ref[1]]
    top = jnp.maximum(jnp.maximum(lse[0], lse[1]), lse[2])
    parts = [jnp.exp(x - top) for x in lse]
    inverse = 1.0 / (parts[0] + parts[1] + parts[2])
    scale = [parts[0] * inverse / total, parts[1] * inverse, parts[2] * inverse]
    for h in range(HEADS):
        row = h // 2 + (PAIRS if h % 2 == 0 else 0)
        at = pl.ds(h * HEAD_DIM, HEAD_DIM)
        mixed = own_ref[0, at] * scale[0][row : row + 1]
        mixed += core_ref[at].astype(jnp.float32) * scale[1][row : row + 1]
        mixed += cross_ref[at].astype(jnp.float32) * scale[2][row : row + 1]
        sum_ref[at] = mixed
    attended = sum_ref[...].T.astype(jnp.bfloat16)
    copies = []
    for c in range(4):
        at = pl.ds(c * 256, 256)
        product = jnp.dot(attended, w_ref[:, at], preferred_element_type=jnp.float32)
        made_ref[:, at] = (features_ref[:, at].astype(jnp.float32) + product).astype(jnp.bfloat16)
        copies.append(pltpu.make_async_copy(made_ref.at[:, at], out_ref.at[:, at], sems.at[c]))
        copies[-1].start()
    for copy in copies:
        copy.wait()


def finish(state, core, cross, out_proj, features):
    m, l, own = state
    lse = finish_first(m, l, cross)
    return pl.pallas_call(
        finish_kernel,
        in_specs=[VMEM] * 7,
        out_specs=pl.BlockSpec(memory_space=pl.ANY),
        out_shape=jax.ShapeDtypeStruct((TILE, D), jnp.bfloat16),
        scratch_shapes=[
            pltpu.VMEM((D, TILE), jnp.float32),
            pltpu.VMEM((TILE, D), jnp.bfloat16),
            pltpu.SemaphoreType.DMA((4,)),
        ],
        compiler_params=PARAMS,
        cost_estimate=pl.CostEstimate(
            flops=2 * TILE * D * D, bytes_accessed=4 * 1024 * 1024, transcendentals=0
        ),
        name="finish",
    )(lse, l, own, core, cross, out_proj, features)


def body(features, norm_gain, in_proj, out_proj, adjacency, counts):
    here, group = lax.axis_index("head"), lax.axis_index("dom")
    group_count, around = lax.axis_size("dom"), lax.axis_size("head")
    gain = norm_gain.reshape(1, D)

    up = [
        (p * around + i, p * around + (i + (-1) ** p) % around)
        for p in range(group_count)
        for i in range(around)
    ]
    up, down = (("dom", "head"), up), (("dom", "head"), [(j, i) for i, j in up])
    swap = [(i, i ^ 1) for i in range(group_count)]
    hop = [(i, i + 1) for i in range(1, group_count - 1, 2)]
    hop = hop + [(j, i) for i, j in hop]

    def tied(x, *others):
        return lax.optimization_barrier((x, *others))[0]

    one = [lax.ppermute(features, *up)]
    parcel, w_query, w_kv = prepare(features, adjacency, counts.reshape(1, NB), in_proj)
    two = [lax.ppermute(tied(features, parcel), *down)]
    from_cross = lax.ppermute(parcel, "dom", hop)
    from_core = lax.ppermute(parcel, "dom", swap)

    one.append(lax.ppermute(tied(one[0], w_query), *up))
    q_own, *kv_a = project([features, one[0]], gain, w_kv, w_query)
    two.append(lax.ppermute(tied(two[0], *kv_a), *down))
    q_near, info = project_near(from_core, from_cross, parcel, gain, w_query)
    kv_a = ((0, -1), *kv_a)
    pair, far = [(q_own, 0, 0), (q_near, 1, 0)], [(q_near, 2, 1)]

    one.append(lax.ppermute(tied(one[1], q_near), *up))
    kv_b = project([two[0], one[1]], gain, w_kv)
    two.append(lax.ppermute(tied(two[1], *kv_b), *down))
    kv_b = ((1, -2), *kv_b)
    far_state = attend(info, far, [kv_a, kv_b])

    one.append(lax.ppermute(tied(one[2], *far_state), *up))
    kv_c = ((2, -3), *project([two[1], one[2]], gain, w_kv))
    kv_d = ((3,), *project([two[2]], gain, w_kv))
    far_state = attend(info, far, [kv_c, kv_d], far_state)

    kv_e = ((4,), *project([tied(one[3], *far_state)], gain, w_kv))
    *_, to_cross = attend(info, far, [kv_e], far_state, last=True)
    cross = lax.ppermute(to_cross, "dom", hop)
    *pair_state, to_core = attend(
        tied(info, to_cross), pair, [kv_a, kv_b, kv_c, kv_d, kv_e], last=True
    )
    core = lax.ppermute(to_core, "dom", swap)
    return finish(pair_state, core, cross, out_proj, features)


def solution(mesh):
    return jax.shard_map(
        body,
        mesh=mesh,
        in_specs=(P(("dom", "head"), None), P(), P(), P(), P("dom", None), P("dom")),
        out_specs=P(("dom", "head"), None),
        check_vma=False,
    )
```

```python
import functools

import jax
import jax.numpy as jnp
from jax import lax
from jax.experimental import pallas as pl
from jax.experimental.pallas import tpu as pltpu
from jax.sharding import PartitionSpec as P

HEADS = 16
HEAD_DIM = 64
TILE = 128
NB = 8
D = 1024
PAIRS = HEADS // 2
STATS = 4 * HEADS
PARTS = 8
LOW = -1e30
epsilon = 1e-05
VMEM = pl.BlockSpec(memory_space=pltpu.VMEM)
SMEM = pl.BlockSpec(memory_space=pltpu.SMEM)
PARAMS = pltpu.CompilerParams(vmem_limit_bytes=40 * 1024 * 1024)


def normed(features, gain):
    wide = features.astype(jnp.float32)
    power = jnp.mean(wide * wide, axis=-1, keepdims=True)
    return (wide * lax.rsqrt(power + epsilon) * gain).astype(jnp.bfloat16)


def prepare_kernel(
    features_ref, adjacency_ref, counts_ref, w_ref, parcel_ref, q_ref, kv_ref, lists_ref, amounts_ref, held_ref, sems
):
    rows = D // PARTS
    copies = [
        pltpu.make_async_copy(features_ref, parcel_ref.at[pl.ds(0, TILE)], sems.at[0]),
        pltpu.make_async_copy(adjacency_ref, lists_ref, sems.at[1]),
        pltpu.make_async_copy(counts_ref, amounts_ref, sems.at[2]),
    ]
    for i in range(PARTS):
        at = pl.ds(i * rows, rows)
        copies.append(pltpu.make_async_copy(w_ref.at[at], held_ref.at[at], sems.at[3 + i]))
    for copy in copies:
        copy.start()
    for copy in copies[:3]:
        copy.wait()
    lists = jnp.concatenate([lists_ref[...], amounts_ref[...], jnp.zeros((7, NB), jnp.int32)], axis=0)
    parcel_ref[pl.ds(TILE, 16)] = jnp.zeros((16, D), jnp.bfloat16)
    parcel_ref[pl.ds(TILE, 16), :NB] = lists.astype(jnp.float32).astype(jnp.bfloat16)
    low = lax.broadcasted_iota(jnp.int32, (rows, 128), 1) < HEAD_DIM
    for i, copy in enumerate(copies[3:]):
        copy.wait()
        at = pl.ds(i * rows, rows)
        for j in range(PAIRS):
            t0, t1, t2 = (held_ref[at, pl.ds(j * 384 + c * 128, 128)] for c in range(3))
            q_ref[at, pl.ds(j * 128, 128)] = jnp.where(low, t0, t1)
            kv_ref[at, pl.ds(j * 128, 128)] = jnp.where(low, t2, t0)
            kv_ref[at, pl.ds(D + j * 128, 128)] = jnp.where(low, t1, t2)


def prepare(features, adjacency, counts, in_proj):
    arrays = (features, adjacency, counts, in_proj)
    return pl.pallas_call(
        prepare_kernel,
        in_specs=[pl.BlockSpec(memory_space=pltpu.HBM)] * 4,
        out_specs=[VMEM] * 3,
        out_shape=[
            jax.ShapeDtypeStruct((TILE + 16, D), jnp.bfloat16),
            jax.ShapeDtypeStruct((D, D), jnp.bfloat16),
            jax.ShapeDtypeStruct((D, 2 * D), jnp.bfloat16),
        ],
        scratch_shapes=[
            pltpu.VMEM((NB, NB), jnp.int32),
            pltpu.VMEM((1, NB), jnp.int32),
            pltpu.VMEM((D, 3 * D), jnp.bfloat16),
            pltpu.SemaphoreType.DMA((3 + PARTS,)),
        ],
        compiler_params=PARAMS,
        cost_estimate=pl.CostEstimate(flops=0, bytes_accessed=12 * 1024 * 1024, transcendentals=0),
        name="prepare",
    )(*(pltpu.with_memory_space_constraint(a, pltpu.HBM) for a in arrays))


def project_queries(rows, w_ref, q_ref, n):
    for c in range(2):
        part = jnp.dot(rows, w_ref[:, c * 512 : (c + 1) * 512], preferred_element_type=jnp.float32)
        part = part.astype(jnp.bfloat16).astype(jnp.float32) * HEAD_DIM ** (-0.5)
        for j in range(4):
            turned = pltpu.roll(part[:, j * 128 : (j + 1) * 128], HEAD_DIM, 1)
            q_ref[n, :, c * 512 + j * 128 : c * 512 + (j + 1) * 128] = turned.astype(jnp.bfloat16)


def needed(ref, n):
    here, group = lax.axis_index("head"), lax.axis_index("dom")
    row = lax.broadcasted_iota(jnp.int32, (16, 128), 0)
    lane = lax.broadcasted_iota(jnp.int32, (16, 128), 1)
    lists = ref[pl.ds(TILE, 16), :128].astype(jnp.float32).astype(jnp.int32)
    count = jnp.where((row == NB) & (lane == here), lists, 0).astype(jnp.float32)
    count = jnp.sum(jnp.sum(count, axis=0, keepdims=True), axis=1, keepdims=True)
    used = (row == here) & (lane < jnp.minimum(count, NB).astype(jnp.int32))
    used = used & (jnp.right_shift(lists, 3) == group)
    bits = jnp.where(used, jnp.left_shift(1, (lists & (NB - 1)) + n * NB), 0).astype(jnp.float32)
    return jnp.sum(jnp.sum(bits, axis=0, keepdims=True), axis=1, keepdims=True)


def near_kernel(core_ref, parcel_ref, gain_ref, w_ref, q_ref, info_ref):
    project_queries(normed(core_ref[:TILE], gain_ref[...]), w_ref, q_ref, 0)
    info = needed(parcel_ref, 0) + needed(core_ref, 1)
    info_ref[...] = jnp.broadcast_to(info, info_ref.shape)


def project_near(core, parcel, gain, w_query):
    return pl.pallas_call(
        near_kernel,
        in_specs=[VMEM] * 4,
        out_specs=[VMEM] * 2,
        out_shape=[
            jax.ShapeDtypeStruct((1, TILE, D), jnp.bfloat16),
            jax.ShapeDtypeStruct((8, 128), jnp.float32),
        ],
        compiler_params=PARAMS,
        cost_estimate=pl.CostEstimate(
            flops=4 * TILE * D * D, bytes_accessed=4 * 1024 * 1024, transcendentals=0
        ),
        name="project_near",
    )(core, parcel, gain, w_query)


def later_kernel(cross_ref, gain_ref, w_ref, info_in, q_ref, info_ref):
    project_queries(normed(cross_ref[:TILE], gain_ref[...]), w_ref, q_ref, 0)
    info_ref[...] = info_in[...] + jnp.broadcast_to(needed(cross_ref, 2), info_ref.shape)


def project_later(cross, gain, w_query, info):
    return pl.pallas_call(
        later_kernel,
        in_specs=[VMEM] * 4,
        out_specs=[VMEM] * 2,
        out_shape=[
            jax.ShapeDtypeStruct((1, TILE, D), jnp.bfloat16),
            jax.ShapeDtypeStruct((8, 128), jnp.float32),
        ],
        compiler_params=PARAMS,
        cost_estimate=pl.CostEstimate(
            flops=2 * TILE * D * D, bytes_accessed=3 * 1024 * 1024, transcendentals=0
        ),
        name="project_later",
    )(cross, gain, w_query, info)


def project_kernel(count, with_query, *refs):
    features, gain_ref, refs = refs[:count], refs[count], refs[count + 1 :]
    if with_query:
        wq_ref, w_ref, q_ref, k_ref, vt_ref, rows_ref = refs
    else:
        w_ref, k_ref, vt_ref, rows_ref = refs
    at = 0
    for ref in features:
        rows_ref[at : at + ref.shape[0]] = normed(ref[...], gain_ref[...])
        at += ref.shape[0]
    if with_query:
        project_queries(rows_ref[:TILE], wq_ref, q_ref, 0)
    for c in range(2):
        at = slice(c * 512, (c + 1) * 512)
        part = jnp.dot(rows_ref[...], w_ref[:, at], preferred_element_type=jnp.float32)
        k_ref[:, at] = part.astype(jnp.bfloat16)
    for c in range(2):
        at, cols = slice(c * 512, (c + 1) * 512), slice(D + c * 512, D + (c + 1) * 512)
        part = jnp.dot(rows_ref[...], w_ref[:, cols], preferred_element_type=jnp.float32)
        vt_ref[at] = part.T.astype(jnp.bfloat16)


def project(arrays, gain, w_kv, w_query=None):
    total, query = sum(a.shape[0] for a in arrays), w_query is not None
    return pl.pallas_call(
        functools.partial(project_kernel, len(arrays), query),
        in_specs=[VMEM] * (len(arrays) + 2 + query),
        out_specs=[VMEM] * (2 + query),
        out_shape=[jax.ShapeDtypeStruct((1, TILE, D), jnp.bfloat16)] * query
        + [
            jax.ShapeDtypeStruct((total, D), jnp.bfloat16),
            jax.ShapeDtypeStruct((D, total), jnp.bfloat16),
        ],
        scratch_shapes=[pltpu.VMEM((total, D), jnp.bfloat16)],
        compiler_params=PARAMS,
        cost_estimate=pl.CostEstimate(
            flops=4 * total * D * D, bytes_accessed=5 * 1024 * 1024, transcendentals=0
        ),
        name="project",
    )(*arrays, gain, *([w_query] * query), w_kv)


def attend_tile(q_ref, k_ref, vt_ref, at, m_ref, l_ref, acc_ref):
    low = lax.broadcasted_iota(jnp.int32, (TILE, 128), 1) < HEAD_DIM
    old, total = m_ref[...], l_ref[...]
    scores, powers, tops, sums = [], [], [], []
    for j in range(PAIRS):
        cols = slice(j * 128, (j + 1) * 128)
        query = q_ref[:, cols]
        zero = jnp.zeros_like(query)
        both = jnp.concatenate([jnp.where(low, query, zero), jnp.where(low, zero, query)], axis=0)
        scores.append(
            lax.dot_general(
                k_ref[at : at + TILE, cols],
                both,
                (((1,), (1,)), ((), ())),
                preferred_element_type=jnp.float32,
            )
        )
    for j in range(PAIRS):
        top = jnp.maximum(old[j : j + 1], jnp.max(scores[j], axis=0, keepdims=True))
        power = jnp.exp(scores[j] - top)
        tops.append(top)
        sums.append(jnp.sum(power, axis=0, keepdims=True))
        powers.append(power.astype(jnp.bfloat16))
    new = jnp.concatenate(tops, axis=0)
    fade = jnp.exp(old - new)
    m_ref[...] = new
    l_ref[...] = total * fade + jnp.concatenate(sums, axis=0)
    for j in range(PAIRS):
        for half, lanes in ((0, slice(TILE, 2 * TILE)), (1, slice(0, TILE))):
            rows = slice(j * 128 + half * HEAD_DIM, j * 128 + (half + 1) * HEAD_DIM)
            mixed = jnp.dot(
                vt_ref[rows, at : at + TILE], powers[j][:, lanes], preferred_element_type=jnp.float32
            )
            acc_ref[rows] = acc_ref[rows] * fade[j : j + 1, lanes] + mixed


def attend_kernel(who, steps, first, last, *refs):
    info_ref, q_refs, refs = refs[0], refs[1 : 1 + len(who)], refs[1 + len(who) :]
    keys, refs = refs[: 2 * len(steps)], refs[2 * len(steps) :]
    if not first:
        refs = refs[3:]
    m_ref, l_ref, acc_ref = refs[:3]
    if first:
        m_ref[...] = jnp.full_like(m_ref, LOW)
        l_ref[...] = jnp.zeros_like(l_ref)
        acc_ref[...] = jnp.zeros_like(acc_ref)
    here, turn = lax.axis_index("head"), 1 - 2 * (lax.axis_index("dom") % 2)
    info = jnp.max(info_ref[...]).astype(jnp.int32)
    for n, (q_ref, (flag, row)) in enumerate(zip(q_refs, who)):
        for s, shifts in enumerate(steps):
            k_ref, vt_ref = keys[2 * s], keys[2 * s + 1]
            for place, shift in enumerate(shifts):
                tile = lax.rem(here + turn * shift + 8, 8)

                @pl.when(jnp.right_shift(info, flag * NB + tile) & 1 != 0)
                def _():
                    attend_tile(
                        q_ref.at[row], k_ref, vt_ref, place * TILE, m_ref.at[n], l_ref.at[n], acc_ref.at[n]
                    )

    if not last:
        return
    n, out_ref = len(who) - 1, refs[3]
    total = l_ref[n]
    some = total > 0
    safe = jnp.where(some, total, 1.0)
    inverse = 1.0 / safe
    lse = jnp.where(some, m_ref[n] + jnp.log(safe), LOW)
    for j in range(PAIRS):
        even, odd = pl.ds(j * 128, HEAD_DIM), pl.ds(j * 128 + HEAD_DIM, HEAD_DIM)
        out_ref[even] = (acc_ref[n, even] * inverse[j : j + 1, TILE:]).astype(jnp.bfloat16)
        out_ref[odd] = (acc_ref[n, odd] * inverse[j : j + 1, :TILE]).astype(jnp.bfloat16)
    stacked = jnp.concatenate([lse[:, :TILE], lse[:, TILE:]], axis=0)
    for c in range(3):
        term = stacked.astype(jnp.bfloat16)
        out_ref[pl.ds(D + c * HEADS, HEADS)] = term
        stacked = stacked - term.astype(jnp.float32)
    out_ref[pl.ds(D + 3 * HEADS, HEADS)] = jnp.ones((HEADS, TILE), jnp.bfloat16)


def attend(info, queries, kv, state=(), last=False):
    who, steps = [q[1:] for q in queries], [shifts for shifts, _, _ in kv]
    arrays = [q[0] for q in queries] + [a for _, k, vt in kv for a in (k, vt)]
    at = 1 + len(arrays)
    return pl.pallas_call(
        functools.partial(attend_kernel, who, steps, not state, last),
        in_specs=[VMEM] * (at + len(state)),
        out_specs=[VMEM] * (4 if last else 3),
        out_shape=[
            jax.ShapeDtypeStruct((len(who), PAIRS, 2 * TILE), jnp.float32),
            jax.ShapeDtypeStruct((len(who), PAIRS, 2 * TILE), jnp.float32),
            jax.ShapeDtypeStruct((len(who), D, TILE), jnp.float32),
        ]
        + [jax.ShapeDtypeStruct((D + STATS, TILE), jnp.bfloat16)] * last,
        input_output_aliases={at + i: i for i in range(len(state))},
        compiler_params=PARAMS,
        cost_estimate=pl.CostEstimate(
            flops=16 * TILE * TILE * D * len(kv), bytes_accessed=4 * 1024 * 1024, transcendentals=0
        ),
        name="attend",
    )(info, *arrays, *state)


def split(x):
    return jnp.concatenate([x[:, :TILE], x[:, TILE:]], axis=0)


def received(ref):
    terms = [ref[pl.ds(D + c * HEADS, HEADS)].astype(jnp.float32) for c in range(4)]
    return jnp.where(terms[3] > 0, terms[0] + terms[1] + terms[2], LOW)


def first_kernel(m_ref, l_ref, cross_ref, lse_ref):
    lse_ref[0] = split(m_ref[0]) + jnp.log(split(l_ref[0]))
    lse_ref[1] = received(cross_ref)


def finish_first(m, l, cross):
    return pl.pallas_call(
        first_kernel,
        in_specs=[VMEM] * 3,
        out_specs=VMEM,
        out_shape=jax.ShapeDtypeStruct((2, HEADS, TILE), jnp.float32),
        compiler_params=PARAMS,
        cost_estimate=pl.CostEstimate(flops=0, bytes_accessed=2 * 1024 * 1024, transcendentals=0),
        name="finish_first",
    )(m, l, cross)


def finish_kernel(lse_ref, l_ref, own_ref, core_ref, cross_ref, w_ref, features_ref, out_ref, sum_ref, made_ref, sems):
    total = split(l_ref[0])
    lse = [lse_ref[0], received(core_ref), lse_ref[1]]
    top = jnp.maximum(jnp.maximum(lse[0], lse[1]), lse[2])
    parts = [jnp.exp(x - top) for x in lse]
    inverse = 1.0 / (parts[0] + parts[1] + parts[2])
    scale = [parts[0] * inverse / total, parts[1] * inverse, parts[2] * inverse]
    for h in range(HEADS):
        row = h // 2 + (PAIRS if h % 2 == 0 else 0)
        at = pl.ds(h * HEAD_DIM, HEAD_DIM)
        mixed = own_ref[0, at] * scale[0][row : row + 1]
        mixed += core_ref[at].astype(jnp.float32) * scale[1][row : row + 1]
        mixed += cross_ref[at].astype(jnp.float32) * scale[2][row : row + 1]
        sum_ref[at] = mixed
    attended = sum_ref[...].T.astype(jnp.bfloat16)
    copies = []
    for c in range(4):
        at = pl.ds(c * 256, 256)
        product = jnp.dot(attended, w_ref[:, at], preferred_element_type=jnp.float32)
        made_ref[:, at] = (features_ref[:, at].astype(jnp.float32) + product).astype(jnp.bfloat16)
        copies.append(pltpu.make_async_copy(made_ref.at[:, at], out_ref.at[:, at], sems.at[c]))
        copies[-1].start()
    for copy in copies:
        copy.wait()


def finish(state, core, cross, out_proj, features):
    m, l, own = state
    lse = finish_first(m, l, cross)
    return pl.pallas_call(
        finish_kernel,
        in_specs=[VMEM] * 7,
        out_specs=pl.BlockSpec(memory_space=pl.ANY),
        out_shape=jax.ShapeDtypeStruct((TILE, D), jnp.bfloat16),
        scratch_shapes=[
            pltpu.VMEM((D, TILE), jnp.float32),
            pltpu.VMEM((TILE, D), jnp.bfloat16),
            pltpu.SemaphoreType.DMA((4,)),
        ],
        compiler_params=PARAMS,
        cost_estimate=pl.CostEstimate(
            flops=2 * TILE * D * D, bytes_accessed=4 * 1024 * 1024, transcendentals=0
        ),
        name="finish",
    )(lse, l, own, core, cross, out_proj, features)


def body(features, norm_gain, in_proj, out_proj, adjacency, counts):
    here, group = lax.axis_index("head"), lax.axis_index("dom")
    group_count, around = lax.axis_size("dom"), lax.axis_size("head")
    gain = norm_gain.reshape(1, D)

    up = [
        (p * around + i, p * around + (i + (-1) ** p) % around)
        for p in range(group_count)
        for i in range(around)
    ]
    up, down = (("dom", "head"), up), (("dom", "head"), [(j, i) for i, j in up])
    swap = [(i, i ^ 1) for i in range(group_count)]
    hop = [(i, i + 1) for i in range(1, group_count - 1, 2)]
    hop = hop + [(j, i) for i, j in hop]

    def tied(x, *others):
        return lax.optimization_barrier((x, *others))[0]

    one = [lax.ppermute(features, *up)]
    parcel, w_query, w_kv = prepare(features, adjacency, counts.reshape(1, NB), in_proj)
    two = [lax.ppermute(tied(features, parcel), *down)]
    from_core = lax.ppermute(parcel, "dom", swap)

    one.append(lax.ppermute(tied(one[0], w_query), *up))
    q_own, *kv_a = project([features, one[0]], gain, w_kv, w_query)
    two.append(lax.ppermute(tied(two[0], *kv_a), *down))
    from_row = lax.ppermute(tied(parcel, one[0]), "dom", hop)
    q_core, info_core = project_near(from_core, parcel, gain, w_query)
    kv_a = ((0, -1), *kv_a)
    pair = [(q_own, 0, 0), (q_core, 1, 0)]

    one.append(lax.ppermute(tied(one[1], q_core), *up))
    kv_b = project([two[0], one[1]], gain, w_kv)
    two.append(lax.ppermute(tied(two[1], *kv_b), *down))
    kv_b = ((1, -2), *kv_b)
    pair_state = attend(info_core, pair, [kv_a])
    q_cross, info = project_later(from_row, gain, w_query, tied(info_core, *pair_state))
    far = [(q_cross, 2, 0)]

    one.append(lax.ppermute(tied(one[2], *pair_state), *up))
    far_state = attend(info, far, [kv_a, kv_b])
    kv_c = ((2, -3), *project([two[1], one[2]], gain, w_kv))
    kv_d = ((3,), *project([two[2]], gain, w_kv))
    far_state = attend(info, far, [kv_c, kv_d], far_state)

    kv_e = ((4,), *project([tied(one[3], *far_state, *pair_state)], gain, w_kv))
    *_, to_cross = attend(info, far, [kv_e], far_state, last=True)
    cross = lax.ppermute(to_cross, "dom", hop)
    *pair_state, to_core = attend(
        info, pair, [kv_b, kv_c, kv_d, kv_e], tied(pair_state, to_cross), last=True
    )
    core = lax.ppermute(to_core, "dom", swap)
    return finish(pair_state, core, cross, out_proj, features)


def solution(mesh):
    return jax.shard_map(
        body,
        mesh=mesh,
        in_specs=(P(("dom", "head"), None), P(), P(), P(), P("dom", None), P("dom")),
        out_specs=P(("dom", "head"), None),
        check_vma=False,
    )
```

```python
import functools

import jax
import jax.numpy as jnp
from jax import lax
from jax.experimental import pallas as pl
from jax.experimental.pallas import tpu as pltpu
from jax.sharding import PartitionSpec as P

HEADS = 16
HEAD_DIM = 64
TILE = 128
NB = 8
D = 1024
PAIRS = HEADS // 2
STATS = 4 * HEADS
PARTS = 8
LOW = -1e30
epsilon = 1e-05
VMEM = pl.BlockSpec(memory_space=pltpu.VMEM)
SMEM = pl.BlockSpec(memory_space=pltpu.SMEM)
PARAMS = pltpu.CompilerParams(vmem_limit_bytes=40 * 1024 * 1024)


def normed(features, gain):
    wide = features.astype(jnp.float32)
    power = jnp.mean(wide * wide, axis=-1, keepdims=True)
    return (wide * lax.rsqrt(power + epsilon) * gain).astype(jnp.bfloat16)


def prepare_kernel(
    features_ref, adjacency_ref, counts_ref, w_ref, parcel_ref, q_ref, kv_ref, lists_ref, amounts_ref, held_ref, sems
):
    rows = D // PARTS
    copies = [
        pltpu.make_async_copy(features_ref, parcel_ref.at[pl.ds(0, TILE)], sems.at[0]),
        pltpu.make_async_copy(adjacency_ref, lists_ref, sems.at[1]),
        pltpu.make_async_copy(counts_ref, amounts_ref, sems.at[2]),
    ]
    for i in range(PARTS):
        at = pl.ds(i * rows, rows)
        copies.append(pltpu.make_async_copy(w_ref.at[at], held_ref.at[at], sems.at[3 + i]))
    for copy in copies:
        copy.start()
    for copy in copies[:3]:
        copy.wait()
    lists = jnp.concatenate([lists_ref[...], amounts_ref[...], jnp.zeros((7, NB), jnp.int32)], axis=0)
    parcel_ref[pl.ds(TILE, 16)] = jnp.zeros((16, D), jnp.bfloat16)
    parcel_ref[pl.ds(TILE, 16), :NB] = lists.astype(jnp.float32).astype(jnp.bfloat16)
    low = lax.broadcasted_iota(jnp.int32, (rows, 128), 1) < HEAD_DIM
    for i, copy in enumerate(copies[3:]):
        copy.wait()
        at = pl.ds(i * rows, rows)
        for j in range(PAIRS):
            t0, t1, t2 = (held_ref[at, pl.ds(j * 384 + c * 128, 128)] for c in range(3))
            q_ref[at, pl.ds(j * 128, 128)] = jnp.where(low, t0, t1)
            kv_ref[at, pl.ds(j * 128, 128)] = jnp.where(low, t2, t0)
            kv_ref[at, pl.ds(D + j * 128, 128)] = jnp.where(low, t1, t2)


def prepare(features, adjacency, counts, in_proj):
    arrays = (features, adjacency, counts, in_proj)
    return pl.pallas_call(
        prepare_kernel,
        in_specs=[pl.BlockSpec(memory_space=pltpu.HBM)] * 4,
        out_specs=[VMEM] * 3,
        out_shape=[
            jax.ShapeDtypeStruct((TILE + 16, D), jnp.bfloat16),
            jax.ShapeDtypeStruct((D, D), jnp.bfloat16),
            jax.ShapeDtypeStruct((D, 2 * D), jnp.bfloat16),
        ],
        scratch_shapes=[
            pltpu.VMEM((NB, NB), jnp.int32),
            pltpu.VMEM((1, NB), jnp.int32),
            pltpu.VMEM((D, 3 * D), jnp.bfloat16),
            pltpu.SemaphoreType.DMA((3 + PARTS,)),
        ],
        compiler_params=PARAMS,
        cost_estimate=pl.CostEstimate(flops=0, bytes_accessed=12 * 1024 * 1024, transcendentals=0),
        name="prepare",
    )(*(pltpu.with_memory_space_constraint(a, pltpu.HBM) for a in arrays))


def project_queries(rows, w_ref, q_ref, n):
    for c in range(2):
        part = jnp.dot(rows, w_ref[:, c * 512 : (c + 1) * 512], preferred_element_type=jnp.float32)
        part = part.astype(jnp.bfloat16).astype(jnp.float32) * HEAD_DIM ** (-0.5)
        for j in range(4):
            turned = pltpu.roll(part[:, j * 128 : (j + 1) * 128], HEAD_DIM, 1)
            q_ref[n, :, c * 512 + j * 128 : c * 512 + (j + 1) * 128] = turned.astype(jnp.bfloat16)


def needed(ref, n):
    here, group = lax.axis_index("head"), lax.axis_index("dom")
    row = lax.broadcasted_iota(jnp.int32, (16, 128), 0)
    lane = lax.broadcasted_iota(jnp.int32, (16, 128), 1)
    lists = ref[pl.ds(TILE, 16), :128].astype(jnp.float32).astype(jnp.int32)
    count = jnp.where((row == NB) & (lane == here), lists, 0).astype(jnp.float32)
    count = jnp.sum(jnp.sum(count, axis=0, keepdims=True), axis=1, keepdims=True)
    used = (row == here) & (lane < jnp.minimum(count, NB).astype(jnp.int32))
    used = used & (jnp.right_shift(lists, 3) == group)
    bits = jnp.where(used, jnp.left_shift(1, (lists & (NB - 1)) + n * NB), 0).astype(jnp.float32)
    return jnp.sum(jnp.sum(bits, axis=0, keepdims=True), axis=1, keepdims=True)


def near_kernel(core_ref, parcel_ref, gain_ref, w_ref, q_ref, info_ref):
    project_queries(normed(core_ref[:TILE], gain_ref[...]), w_ref, q_ref, 0)
    info = needed(parcel_ref, 0) + needed(core_ref, 1)
    info_ref[...] = jnp.broadcast_to(info, info_ref.shape)


def project_near(core, parcel, gain, w_query):
    return pl.pallas_call(
        near_kernel,
        in_specs=[VMEM] * 4,
        out_specs=[VMEM] * 2,
        out_shape=[
            jax.ShapeDtypeStruct((1, TILE, D), jnp.bfloat16),
            jax.ShapeDtypeStruct((8, 128), jnp.float32),
        ],
        compiler_params=PARAMS,
        cost_estimate=pl.CostEstimate(
            flops=4 * TILE * D * D, bytes_accessed=4 * 1024 * 1024, transcendentals=0
        ),
        name="project_near",
    )(core, parcel, gain, w_query)


def later_kernel(cross_ref, gain_ref, w_ref, info_in, q_ref, info_ref):
    project_queries(normed(cross_ref[:TILE], gain_ref[...]), w_ref, q_ref, 0)
    info_ref[...] = info_in[...] + jnp.broadcast_to(needed(cross_ref, 2), info_ref.shape)


def project_later(cross, gain, w_query, info):
    return pl.pallas_call(
        later_kernel,
        in_specs=[VMEM] * 4,
        out_specs=[VMEM] * 2,
        out_shape=[
            jax.ShapeDtypeStruct((1, TILE, D), jnp.bfloat16),
            jax.ShapeDtypeStruct((8, 128), jnp.float32),
        ],
        compiler_params=PARAMS,
        cost_estimate=pl.CostEstimate(
            flops=2 * TILE * D * D, bytes_accessed=3 * 1024 * 1024, transcendentals=0
        ),
        name="project_later",
    )(cross, gain, w_query, info)


def project_kernel(count, with_query, *refs):
    features, gain_ref, refs = refs[:count], refs[count], refs[count + 1 :]
    if with_query:
        wq_ref, w_ref, q_ref, k_ref, vt_ref, rows_ref = refs
    else:
        w_ref, k_ref, vt_ref, rows_ref = refs
    at = 0
    for ref in features:
        rows_ref[at : at + ref.shape[0]] = normed(ref[...], gain_ref[...])
        at += ref.shape[0]
    if with_query:
        project_queries(rows_ref[:TILE], wq_ref, q_ref, 0)
    for c in range(2):
        at = slice(c * 512, (c + 1) * 512)
        part = jnp.dot(rows_ref[...], w_ref[:, at], preferred_element_type=jnp.float32)
        k_ref[:, at] = part.astype(jnp.bfloat16)
    for c in range(2):
        at, cols = slice(c * 512, (c + 1) * 512), slice(D + c * 512, D + (c + 1) * 512)
        part = jnp.dot(rows_ref[...], w_ref[:, cols], preferred_element_type=jnp.float32)
        vt_ref[at] = part.T.astype(jnp.bfloat16)


def project(arrays, gain, w_kv, w_query=None):
    total, query = sum(a.shape[0] for a in arrays), w_query is not None
    return pl.pallas_call(
        functools.partial(project_kernel, len(arrays), query),
        in_specs=[VMEM] * (len(arrays) + 2 + query),
        out_specs=[VMEM] * (2 + query),
        out_shape=[jax.ShapeDtypeStruct((1, TILE, D), jnp.bfloat16)] * query
        + [
            jax.ShapeDtypeStruct((total, D), jnp.bfloat16),
            jax.ShapeDtypeStruct((D, total), jnp.bfloat16),
        ],
        scratch_shapes=[pltpu.VMEM((total, D), jnp.bfloat16)],
        compiler_params=PARAMS,
        cost_estimate=pl.CostEstimate(
            flops=4 * total * D * D, bytes_accessed=5 * 1024 * 1024, transcendentals=0
        ),
        name="project",
    )(*arrays, gain, *([w_query] * query), w_kv)


def attend_tile(q_ref, k_ref, vt_ref, at, m_ref, l_ref, acc_ref):
    low = lax.broadcasted_iota(jnp.int32, (TILE, 128), 1) < HEAD_DIM
    old, total = m_ref[...], l_ref[...]
    scores, powers, tops, sums = [], [], [], []
    for j in range(PAIRS):
        cols = slice(j * 128, (j + 1) * 128)
        query = q_ref[:, cols]
        zero = jnp.zeros_like(query)
        both = jnp.concatenate([jnp.where(low, query, zero), jnp.where(low, zero, query)], axis=0)
        scores.append(
            lax.dot_general(
                k_ref[at : at + TILE, cols],
                both,
                (((1,), (1,)), ((), ())),
                preferred_element_type=jnp.float32,
            )
        )
    for j in range(PAIRS):
        top = jnp.maximum(old[j : j + 1], jnp.max(scores[j], axis=0, keepdims=True))
        power = jnp.exp(scores[j] - top)
        tops.append(top)
        sums.append(jnp.sum(power, axis=0, keepdims=True))
        powers.append(power.astype(jnp.bfloat16))
    new = jnp.concatenate(tops, axis=0)
    fade = jnp.exp(old - new)
    m_ref[...] = new
    l_ref[...] = total * fade + jnp.concatenate(sums, axis=0)
    for j in range(PAIRS):
        for half, lanes in ((0, slice(TILE, 2 * TILE)), (1, slice(0, TILE))):
            rows = slice(j * 128 + half * HEAD_DIM, j * 128 + (half + 1) * HEAD_DIM)
            mixed = jnp.dot(
                vt_ref[rows, at : at + TILE], powers[j][:, lanes], preferred_element_type=jnp.float32
            )
            acc_ref[rows] = acc_ref[rows] * fade[j : j + 1, lanes] + mixed


def attend_kernel(who, steps, first, last, *refs):
    info_ref, q_refs, refs = refs[0], refs[1 : 1 + len(who)], refs[1 + len(who) :]
    keys, refs = refs[: 2 * len(steps)], refs[2 * len(steps) :]
    if not first:
        refs = refs[3:]
    m_ref, l_ref, acc_ref = refs[:3]
    if first:
        m_ref[...] = jnp.full_like(m_ref, LOW)
        l_ref[...] = jnp.zeros_like(l_ref)
        acc_ref[...] = jnp.zeros_like(acc_ref)
    here, turn = lax.axis_index("head"), 1 - 2 * (lax.axis_index("dom") % 2)
    info = jnp.max(info_ref[...]).astype(jnp.int32)
    for n, (q_ref, (flag, row)) in enumerate(zip(q_refs, who)):
        for s, shifts in enumerate(steps):
            k_ref, vt_ref = keys[2 * s], keys[2 * s + 1]
            for place, shift in enumerate(shifts):
                tile = lax.rem(here + turn * shift + 8, 8)

                @pl.when(jnp.right_shift(info, flag * NB + tile) & 1 != 0)
                def _():
                    attend_tile(
                        q_ref.at[row], k_ref, vt_ref, place * TILE, m_ref.at[n], l_ref.at[n], acc_ref.at[n]
                    )

    if not last:
        return
    n, out_ref = len(who) - 1, refs[3]
    total = l_ref[n]
    some = total > 0
    safe = jnp.where(some, total, 1.0)
    inverse = 1.0 / safe
    lse = jnp.where(some, m_ref[n] + jnp.log(safe), LOW)
    for j in range(PAIRS):
        even, odd = pl.ds(j * 128, HEAD_DIM), pl.ds(j * 128 + HEAD_DIM, HEAD_DIM)
        out_ref[even] = (acc_ref[n, even] * inverse[j : j + 1, TILE:]).astype(jnp.bfloat16)
        out_ref[odd] = (acc_ref[n, odd] * inverse[j : j + 1, :TILE]).astype(jnp.bfloat16)
    stacked = jnp.concatenate([lse[:, :TILE], lse[:, TILE:]], axis=0)
    for c in range(3):
        term = stacked.astype(jnp.bfloat16)
        out_ref[pl.ds(D + c * HEADS, HEADS)] = term
        stacked = stacked - term.astype(jnp.float32)
    out_ref[pl.ds(D + 3 * HEADS, HEADS)] = jnp.ones((HEADS, TILE), jnp.bfloat16)


def attend(info, queries, kv, state=(), last=False):
    who, steps = [q[1:] for q in queries], [shifts for shifts, _, _ in kv]
    arrays = [q[0] for q in queries] + [a for _, k, vt in kv for a in (k, vt)]
    at = 1 + len(arrays)
    return pl.pallas_call(
        functools.partial(attend_kernel, who, steps, not state, last),
        in_specs=[VMEM] * (at + len(state)),
        out_specs=[VMEM] * (4 if last else 3),
        out_shape=[
            jax.ShapeDtypeStruct((len(who), PAIRS, 2 * TILE), jnp.float32),
            jax.ShapeDtypeStruct((len(who), PAIRS, 2 * TILE), jnp.float32),
            jax.ShapeDtypeStruct((len(who), D, TILE), jnp.float32),
        ]
        + [jax.ShapeDtypeStruct((D + STATS, TILE), jnp.bfloat16)] * last,
        input_output_aliases={at + i: i for i in range(len(state))},
        compiler_params=PARAMS,
        cost_estimate=pl.CostEstimate(
            flops=16 * TILE * TILE * D * len(kv), bytes_accessed=4 * 1024 * 1024, transcendentals=0
        ),
        name="attend",
    )(info, *arrays, *state)


def split(x):
    return jnp.concatenate([x[:, :TILE], x[:, TILE:]], axis=0)


def received(ref):
    terms = [ref[pl.ds(D + c * HEADS, HEADS)].astype(jnp.float32) for c in range(4)]
    return jnp.where(terms[3] > 0, terms[0] + terms[1] + terms[2], LOW)


def first_kernel(m_ref, l_ref, cross_ref, lse_ref):
    lse_ref[0] = split(m_ref[0]) + jnp.log(split(l_ref[0]))
    lse_ref[1] = received(cross_ref)


def finish_first(m, l, cross):
    return pl.pallas_call(
        first_kernel,
        in_specs=[VMEM] * 3,
        out_specs=VMEM,
        out_shape=jax.ShapeDtypeStruct((2, HEADS, TILE), jnp.float32),
        compiler_params=PARAMS,
        cost_estimate=pl.CostEstimate(flops=0, bytes_accessed=2 * 1024 * 1024, transcendentals=0),
        name="finish_first",
    )(m, l, cross)


def finish_kernel(lse_ref, l_ref, own_ref, core_ref, cross_ref, w_ref, features_ref, out_ref, sum_ref, made_ref, sems):
    total = split(l_ref[0])
    lse = [lse_ref[0], received(core_ref), lse_ref[1]]
    top = jnp.maximum(jnp.maximum(lse[0], lse[1]), lse[2])
    parts = [jnp.exp(x - top) for x in lse]
    inverse = 1.0 / (parts[0] + parts[1] + parts[2])
    scale = [parts[0] * inverse / total, parts[1] * inverse, parts[2] * inverse]
    for h in range(HEADS):
        row = h // 2 + (PAIRS if h % 2 == 0 else 0)
        at = pl.ds(h * HEAD_DIM, HEAD_DIM)
        mixed = own_ref[0, at] * scale[0][row : row + 1]
        mixed += core_ref[at].astype(jnp.float32) * scale[1][row : row + 1]
        mixed += cross_ref[at].astype(jnp.float32) * scale[2][row : row + 1]
        sum_ref[at] = mixed
    attended = sum_ref[...].T.astype(jnp.bfloat16)
    copies = []
    for c in range(4):
        at = pl.ds(c * 256, 256)
        product = jnp.dot(attended, w_ref[:, at], preferred_element_type=jnp.float32)
        made_ref[:, at] = (features_ref[:, at].astype(jnp.float32) + product).astype(jnp.bfloat16)
        copies.append(pltpu.make_async_copy(made_ref.at[:, at], out_ref.at[:, at], sems.at[c]))
        copies[-1].start()
    for copy in copies:
        copy.wait()


def finish(state, core, cross, out_proj, features):
    m, l, own = state
    lse = finish_first(m, l, cross)
    return pl.pallas_call(
        finish_kernel,
        in_specs=[VMEM] * 7,
        out_specs=pl.BlockSpec(memory_space=pl.ANY),
        out_shape=jax.ShapeDtypeStruct((TILE, D), jnp.bfloat16),
        scratch_shapes=[
            pltpu.VMEM((D, TILE), jnp.float32),
            pltpu.VMEM((TILE, D), jnp.bfloat16),
            pltpu.SemaphoreType.DMA((4,)),
        ],
        compiler_params=PARAMS,
        cost_estimate=pl.CostEstimate(
            flops=2 * TILE * D * D, bytes_accessed=4 * 1024 * 1024, transcendentals=0
        ),
        name="finish",
    )(lse, l, own, core, cross, out_proj, features)


def body(features, norm_gain, in_proj, out_proj, adjacency, counts):
    here, group = lax.axis_index("head"), lax.axis_index("dom")
    group_count, around = lax.axis_size("dom"), lax.axis_size("head")
    gain = norm_gain.reshape(1, D)

    up = [
        (p * around + i, p * around + (i + (-1) ** p) % around)
        for p in range(group_count)
        for i in range(around)
    ]
    up, down = (("dom", "head"), up), (("dom", "head"), [(j, i) for i, j in up])
    swap = [(i, i ^ 1) for i in range(group_count)]
    hop = [(i, i + 1) for i in range(1, group_count - 1, 2)]
    hop = hop + [(j, i) for i, j in hop]

    def tied(x, *others):
        return lax.optimization_barrier((x, *others))[0]

    one = [lax.ppermute(features, *up)]
    parcel, w_query, w_kv = prepare(features, adjacency, counts.reshape(1, NB), in_proj)
    two = [lax.ppermute(tied(features, parcel), *down)]
    from_core = lax.ppermute(parcel, "dom", swap)

    one.append(lax.ppermute(tied(one[0], w_query), *up))
    q_own, *kv_a = project([features, one[0]], gain, w_kv, w_query)
    two.append(lax.ppermute(tied(two[0], *kv_a), *down))
    from_row = lax.ppermute(tied(parcel, one[0]), "dom", hop)
    q_core, info_core = project_near(from_core, parcel, gain, w_query)
    kv_a = ((0, -1), *kv_a)
    pair = [(q_own, 0, 0), (q_core, 1, 0)]

    one.append(lax.ppermute(tied(one[1], q_core), *up))
    kv_b = project([two[0], one[1]], gain, w_kv)
    two.append(lax.ppermute(tied(two[1], *kv_b), *down))
    kv_b = ((1, -2), *kv_b)
    pair_state = attend(info_core, pair, [kv_a])
    q_cross, info = project_later(from_row, gain, w_query, tied(info_core, *pair_state))
    far = [(q_cross, 2, 0)]

    one.append(lax.ppermute(tied(one[2], kv_b[1]), *up))
    far_state = attend(info, far, [kv_a, kv_b])
    kv_c = ((2, -3), *project([two[1], one[2]], gain, w_kv))
    kv_d = ((3,), *project([two[2]], gain, w_kv))
    far_state = attend(info, far, [kv_c, kv_d], far_state)

    kv_e = ((4,), *project([tied(one[3], *far_state, *pair_state)], gain, w_kv))
    *_, to_cross = attend(info, far, [kv_e], far_state, last=True)
    cross = lax.ppermute(to_cross, "dom", hop)
    *pair_state, to_core = attend(
        info, pair, [kv_b, kv_c, kv_d, kv_e], tied(pair_state, to_cross), last=True
    )
    core = lax.ppermute(to_core, "dom", swap)
    return finish(pair_state, core, cross, out_proj, features)


def solution(mesh):
    return jax.shard_map(
        body,
        mesh=mesh,
        in_specs=(P(("dom", "head"), None), P(), P(), P(), P("dom", None), P("dom")),
        out_specs=P(("dom", "head"), None),
        check_vma=False,
    )
```

```python
import functools

import jax
import jax.numpy as jnp
from jax import lax
from jax.experimental import pallas as pl
from jax.experimental.pallas import tpu as pltpu
from jax.sharding import PartitionSpec as P

HEADS = 16
HEAD_DIM = 64
TILE = 128
NB = 8
D = 1024
PAIRS = HEADS // 2
STATS = 4 * HEADS
PARTS = 8
LOW = -1e30
epsilon = 1e-05
VMEM = pl.BlockSpec(memory_space=pltpu.VMEM)
SMEM = pl.BlockSpec(memory_space=pltpu.SMEM)
PARAMS = pltpu.CompilerParams(vmem_limit_bytes=40 * 1024 * 1024)


def normed(features, gain):
    wide = features.astype(jnp.float32)
    power = jnp.mean(wide * wide, axis=-1, keepdims=True)
    return (wide * lax.rsqrt(power + epsilon) * gain).astype(jnp.bfloat16)


def prepare_kernel(
    features_ref, adjacency_ref, counts_ref, w_ref, parcel_ref, q_ref, kv_ref, lists_ref, amounts_ref, held_ref, sems
):
    rows = D // PARTS
    copies = [
        pltpu.make_async_copy(features_ref, parcel_ref.at[pl.ds(0, TILE)], sems.at[0]),
        pltpu.make_async_copy(adjacency_ref, lists_ref, sems.at[1]),
        pltpu.make_async_copy(counts_ref, amounts_ref, sems.at[2]),
    ]
    for i in range(PARTS):
        at = pl.ds(i * rows, rows)
        copies.append(pltpu.make_async_copy(w_ref.at[at], held_ref.at[at], sems.at[3 + i]))
    for copy in copies:
        copy.start()
    for copy in copies[:3]:
        copy.wait()
    lists = jnp.concatenate([lists_ref[...], amounts_ref[...], jnp.zeros((7, NB), jnp.int32)], axis=0)
    parcel_ref[pl.ds(TILE, 16)] = jnp.zeros((16, D), jnp.bfloat16)
    parcel_ref[pl.ds(TILE, 16), :NB] = lists.astype(jnp.float32).astype(jnp.bfloat16)
    low = lax.broadcasted_iota(jnp.int32, (rows, 128), 1) < HEAD_DIM
    for i, copy in enumerate(copies[3:]):
        copy.wait()
        at = pl.ds(i * rows, rows)
        for j in range(PAIRS):
            t0, t1, t2 = (held_ref[at, pl.ds(j * 384 + c * 128, 128)] for c in range(3))
            q_ref[at, pl.ds(j * 128, 128)] = jnp.where(low, t0, t1)
            kv_ref[at, pl.ds(j * 128, 128)] = jnp.where(low, t2, t0)
            kv_ref[at, pl.ds(D + j * 128, 128)] = jnp.where(low, t1, t2)


def prepare(features, adjacency, counts, in_proj):
    arrays = (features, adjacency, counts, in_proj)
    return pl.pallas_call(
        prepare_kernel,
        in_specs=[pl.BlockSpec(memory_space=pltpu.HBM)] * 4,
        out_specs=[VMEM] * 3,
        out_shape=[
            jax.ShapeDtypeStruct((TILE + 16, D), jnp.bfloat16),
            jax.ShapeDtypeStruct((D, D), jnp.bfloat16),
            jax.ShapeDtypeStruct((D, 2 * D), jnp.bfloat16),
        ],
        scratch_shapes=[
            pltpu.VMEM((NB, NB), jnp.int32),
            pltpu.VMEM((1, NB), jnp.int32),
            pltpu.VMEM((D, 3 * D), jnp.bfloat16),
            pltpu.SemaphoreType.DMA((3 + PARTS,)),
        ],
        compiler_params=PARAMS,
        cost_estimate=pl.CostEstimate(flops=0, bytes_accessed=12 * 1024 * 1024, transcendentals=0),
        name="prepare",
    )(*(pltpu.with_memory_space_constraint(a, pltpu.HBM) for a in arrays))


def project_queries(rows, w_ref, q_ref, n):
    for c in range(2):
        part = jnp.dot(rows, w_ref[:, c * 512 : (c + 1) * 512], preferred_element_type=jnp.float32)
        part = part.astype(jnp.bfloat16).astype(jnp.float32) * HEAD_DIM ** (-0.5)
        for j in range(4):
            turned = pltpu.roll(part[:, j * 128 : (j + 1) * 128], HEAD_DIM, 1)
            q_ref[n, :, c * 512 + j * 128 : c * 512 + (j + 1) * 128] = turned.astype(jnp.bfloat16)


def needed(ref, n):
    here, group = lax.axis_index("head"), lax.axis_index("dom")
    row = lax.broadcasted_iota(jnp.int32, (16, 128), 0)
    lane = lax.broadcasted_iota(jnp.int32, (16, 128), 1)
    lists = ref[pl.ds(TILE, 16), :128].astype(jnp.float32).astype(jnp.int32)
    count = jnp.where((row == NB) & (lane == here), lists, 0).astype(jnp.float32)
    count = jnp.sum(jnp.sum(count, axis=0, keepdims=True), axis=1, keepdims=True)
    used = (row == here) & (lane < jnp.minimum(count, NB).astype(jnp.int32))
    used = used & (jnp.right_shift(lists, 3) == group)
    bits = jnp.where(used, jnp.left_shift(1, (lists & (NB - 1)) + n * NB), 0).astype(jnp.float32)
    return jnp.sum(jnp.sum(bits, axis=0, keepdims=True), axis=1, keepdims=True)


def near_kernel(core_ref, parcel_ref, gain_ref, w_ref, q_ref, info_ref):
    project_queries(normed(core_ref[:TILE], gain_ref[...]), w_ref, q_ref, 0)
    info = needed(parcel_ref, 0) + needed(core_ref, 1)
    info_ref[...] = jnp.broadcast_to(info, info_ref.shape)


def project_near(core, parcel, gain, w_query):
    return pl.pallas_call(
        near_kernel,
        in_specs=[VMEM] * 4,
        out_specs=[VMEM] * 2,
        out_shape=[
            jax.ShapeDtypeStruct((1, TILE, D), jnp.bfloat16),
            jax.ShapeDtypeStruct((8, 128), jnp.float32),
        ],
        compiler_params=PARAMS,
        cost_estimate=pl.CostEstimate(
            flops=4 * TILE * D * D, bytes_accessed=4 * 1024 * 1024, transcendentals=0
        ),
        name="project_near",
    )(core, parcel, gain, w_query)


def later_kernel(cross_ref, gain_ref, w_ref, info_in, q_ref, info_ref):
    project_queries(normed(cross_ref[:TILE], gain_ref[...]), w_ref, q_ref, 0)
    info_ref[...] = info_in[...] + jnp.broadcast_to(needed(cross_ref, 2), info_ref.shape)


def project_later(cross, gain, w_query, info):
    return pl.pallas_call(
        later_kernel,
        in_specs=[VMEM] * 4,
        out_specs=[VMEM] * 2,
        out_shape=[
            jax.ShapeDtypeStruct((1, TILE, D), jnp.bfloat16),
            jax.ShapeDtypeStruct((8, 128), jnp.float32),
        ],
        compiler_params=PARAMS,
        cost_estimate=pl.CostEstimate(
            flops=2 * TILE * D * D, bytes_accessed=3 * 1024 * 1024, transcendentals=0
        ),
        name="project_later",
    )(cross, gain, w_query, info)


def project_kernel(count, with_query, *refs):
    features, gain_ref, refs = refs[:count], refs[count], refs[count + 1 :]
    if with_query:
        wq_ref, w_ref, q_ref, k_ref, vt_ref, rows_ref = refs
    else:
        w_ref, k_ref, vt_ref, rows_ref = refs
    at = 0
    for ref in features:
        rows_ref[at : at + ref.shape[0]] = normed(ref[...], gain_ref[...])
        at += ref.shape[0]
    if with_query:
        project_queries(rows_ref[:TILE], wq_ref, q_ref, 0)
    for c in range(2):
        at = slice(c * 512, (c + 1) * 512)
        part = jnp.dot(rows_ref[...], w_ref[:, at], preferred_element_type=jnp.float32)
        k_ref[:, at] = part.astype(jnp.bfloat16)
    for c in range(2):
        at, cols = slice(c * 512, (c + 1) * 512), slice(D + c * 512, D + (c + 1) * 512)
        part = jnp.dot(rows_ref[...], w_ref[:, cols], preferred_element_type=jnp.float32)
        vt_ref[at] = part.T.astype(jnp.bfloat16)


def project(arrays, gain, w_kv, w_query=None):
    total, query = sum(a.shape[0] for a in arrays), w_query is not None
    return pl.pallas_call(
        functools.partial(project_kernel, len(arrays), query),
        in_specs=[VMEM] * (len(arrays) + 2 + query),
        out_specs=[VMEM] * (2 + query),
        out_shape=[jax.ShapeDtypeStruct((1, TILE, D), jnp.bfloat16)] * query
        + [
            jax.ShapeDtypeStruct((total, D), jnp.bfloat16),
            jax.ShapeDtypeStruct((D, total), jnp.bfloat16),
        ],
        scratch_shapes=[pltpu.VMEM((total, D), jnp.bfloat16)],
        compiler_params=PARAMS,
        cost_estimate=pl.CostEstimate(
            flops=4 * total * D * D, bytes_accessed=5 * 1024 * 1024, transcendentals=0
        ),
        name="project",
    )(*arrays, gain, *([w_query] * query), w_kv)


def attend_tile(q_ref, k_ref, vt_ref, at, m_ref, l_ref, acc_ref):
    low = lax.broadcasted_iota(jnp.int32, (TILE, 128), 1) < HEAD_DIM
    old, total = m_ref[...], l_ref[...]
    scores, powers, tops, sums = [], [], [], []
    for j in range(PAIRS):
        cols = slice(j * 128, (j + 1) * 128)
        query = q_ref[:, cols]
        zero = jnp.zeros_like(query)
        both = jnp.concatenate([jnp.where(low, query, zero), jnp.where(low, zero, query)], axis=0)
        scores.append(
            lax.dot_general(
                k_ref[at : at + TILE, cols],
                both,
                (((1,), (1,)), ((), ())),
                preferred_element_type=jnp.float32,
            )
        )
    for j in range(PAIRS):
        top = jnp.maximum(old[j : j + 1], jnp.max(scores[j], axis=0, keepdims=True))
        power = jnp.exp(scores[j] - top)
        tops.append(top)
        sums.append(jnp.sum(power, axis=0, keepdims=True))
        powers.append(power.astype(jnp.bfloat16))
    new = jnp.concatenate(tops, axis=0)
    fade = jnp.exp(old - new)
    m_ref[...] = new
    l_ref[...] = total * fade + jnp.concatenate(sums, axis=0)
    for j in range(PAIRS):
        for half, lanes in ((0, slice(TILE, 2 * TILE)), (1, slice(0, TILE))):
            rows = slice(j * 128 + half * HEAD_DIM, j * 128 + (half + 1) * HEAD_DIM)
            mixed = jnp.dot(
                vt_ref[rows, at : at + TILE], powers[j][:, lanes], preferred_element_type=jnp.float32
            )
            acc_ref[rows] = acc_ref[rows] * fade[j : j + 1, lanes] + mixed


def attend_kernel(who, steps, first, last, *refs):
    info_ref, q_refs, refs = refs[0], refs[1 : 1 + len(who)], refs[1 + len(who) :]
    keys, refs = refs[: 2 * len(steps)], refs[2 * len(steps) :]
    if not first:
        refs = refs[3:]
    m_ref, l_ref, acc_ref = refs[:3]
    if first:
        m_ref[...] = jnp.full_like(m_ref, LOW)
        l_ref[...] = jnp.zeros_like(l_ref)
        acc_ref[...] = jnp.zeros_like(acc_ref)
    here, turn = lax.axis_index("head"), 1 - 2 * (lax.axis_index("dom") % 2)
    info = jnp.max(info_ref[...]).astype(jnp.int32)
    for n, (q_ref, (flag, row)) in enumerate(zip(q_refs, who)):
        for s, shifts in enumerate(steps):
            k_ref, vt_ref = keys[2 * s], keys[2 * s + 1]
            for place, shift in enumerate(shifts):
                tile = lax.rem(here + turn * shift + 8, 8)

                @pl.when(jnp.right_shift(info, flag * NB + tile) & 1 != 0)
                def _():
                    attend_tile(
                        q_ref.at[row], k_ref, vt_ref, place * TILE, m_ref.at[n], l_ref.at[n], acc_ref.at[n]
                    )

    if not last:
        return
    n, out_ref = len(who) - 1, refs[3]
    total = l_ref[n]
    some = total > 0
    safe = jnp.where(some, total, 1.0)
    inverse = 1.0 / safe
    lse = jnp.where(some, m_ref[n] + jnp.log(safe), LOW)
    for j in range(PAIRS):
        even, odd = pl.ds(j * 128, HEAD_DIM), pl.ds(j * 128 + HEAD_DIM, HEAD_DIM)
        out_ref[even] = (acc_ref[n, even] * inverse[j : j + 1, TILE:]).astype(jnp.bfloat16)
        out_ref[odd] = (acc_ref[n, odd] * inverse[j : j + 1, :TILE]).astype(jnp.bfloat16)
    stacked = jnp.concatenate([lse[:, :TILE], lse[:, TILE:]], axis=0)
    for c in range(3):
        term = stacked.astype(jnp.bfloat16)
        out_ref[pl.ds(D + c * HEADS, HEADS)] = term
        stacked = stacked - term.astype(jnp.float32)
    out_ref[pl.ds(D + 3 * HEADS, HEADS)] = jnp.ones((HEADS, TILE), jnp.bfloat16)


def attend(info, queries, kv, state=(), last=False):
    who, steps = [q[1:] for q in queries], [shifts for shifts, _, _ in kv]
    arrays = [q[0] for q in queries] + [a for _, k, vt in kv for a in (k, vt)]
    at = 1 + len(arrays)
    return pl.pallas_call(
        functools.partial(attend_kernel, who, steps, not state, last),
        in_specs=[VMEM] * (at + len(state)),
        out_specs=[VMEM] * (4 if last else 3),
        out_shape=[
            jax.ShapeDtypeStruct((len(who), PAIRS, 2 * TILE), jnp.float32),
            jax.ShapeDtypeStruct((len(who), PAIRS, 2 * TILE), jnp.float32),
            jax.ShapeDtypeStruct((len(who), D, TILE), jnp.float32),
        ]
        + [jax.ShapeDtypeStruct((D + STATS, TILE), jnp.bfloat16)] * last,
        input_output_aliases={at + i: i for i in range(len(state))},
        compiler_params=PARAMS,
        cost_estimate=pl.CostEstimate(
            flops=16 * TILE * TILE * D * len(kv), bytes_accessed=4 * 1024 * 1024, transcendentals=0
        ),
        name="attend",
    )(info, *arrays, *state)


def split(x):
    return jnp.concatenate([x[:, :TILE], x[:, TILE:]], axis=0)


def received(ref):
    terms = [ref[pl.ds(D + c * HEADS, HEADS)].astype(jnp.float32) for c in range(4)]
    return jnp.where(terms[3] > 0, terms[0] + terms[1] + terms[2], LOW)


def first_kernel(m_ref, l_ref, cross_ref, lse_ref):
    lse_ref[0] = split(m_ref[0]) + jnp.log(split(l_ref[0]))
    lse_ref[1] = received(cross_ref)


def finish_first(m, l, cross):
    return pl.pallas_call(
        first_kernel,
        in_specs=[VMEM] * 3,
        out_specs=VMEM,
        out_shape=jax.ShapeDtypeStruct((2, HEADS, TILE), jnp.float32),
        compiler_params=PARAMS,
        cost_estimate=pl.CostEstimate(flops=0, bytes_accessed=2 * 1024 * 1024, transcendentals=0),
        name="finish_first",
    )(m, l, cross)


def finish_kernel(lse_ref, l_ref, own_ref, core_ref, cross_ref, w_ref, features_ref, out_ref, sum_ref, made_ref, sems):
    total = split(l_ref[0])
    lse = [lse_ref[0], received(core_ref), lse_ref[1]]
    top = jnp.maximum(jnp.maximum(lse[0], lse[1]), lse[2])
    parts = [jnp.exp(x - top) for x in lse]
    inverse = 1.0 / (parts[0] + parts[1] + parts[2])
    scale = [parts[0] * inverse / total, parts[1] * inverse, parts[2] * inverse]
    for h in range(HEADS):
        row = h // 2 + (PAIRS if h % 2 == 0 else 0)
        at = pl.ds(h * HEAD_DIM, HEAD_DIM)
        mixed = own_ref[0, at] * scale[0][row : row + 1]
        mixed += core_ref[at].astype(jnp.float32) * scale[1][row : row + 1]
        mixed += cross_ref[at].astype(jnp.float32) * scale[2][row : row + 1]
        sum_ref[at] = mixed
    attended = sum_ref[...].T.astype(jnp.bfloat16)
    copies = []
    for c in range(4):
        at = pl.ds(c * 256, 256)
        product = jnp.dot(attended, w_ref[:, at], preferred_element_type=jnp.float32)
        made_ref[:, at] = (features_ref[:, at].astype(jnp.float32) + product).astype(jnp.bfloat16)
        copies.append(pltpu.make_async_copy(made_ref.at[:, at], out_ref.at[:, at], sems.at[c]))
        copies[-1].start()
    for copy in copies:
        copy.wait()


def finish(state, core, cross, out_proj, features):
    m, l, own = state
    lse = finish_first(m, l, cross)
    return pl.pallas_call(
        finish_kernel,
        in_specs=[VMEM] * 7,
        out_specs=pl.BlockSpec(memory_space=pl.ANY),
        out_shape=jax.ShapeDtypeStruct((TILE, D), jnp.bfloat16),
        scratch_shapes=[
            pltpu.VMEM((D, TILE), jnp.float32),
            pltpu.VMEM((TILE, D), jnp.bfloat16),
            pltpu.SemaphoreType.DMA((4,)),
        ],
        compiler_params=PARAMS,
        cost_estimate=pl.CostEstimate(
            flops=2 * TILE * D * D, bytes_accessed=4 * 1024 * 1024, transcendentals=0
        ),
        name="finish",
    )(lse, l, own, core, cross, out_proj, features)


def body(features, norm_gain, in_proj, out_proj, adjacency, counts):
    here, group = lax.axis_index("head"), lax.axis_index("dom")
    group_count, around = lax.axis_size("dom"), lax.axis_size("head")
    gain = norm_gain.reshape(1, D)

    up = [
        (p * around + i, p * around + (i + (-1) ** p) % around)
        for p in range(group_count)
        for i in range(around)
    ]
    up, down = (("dom", "head"), up), (("dom", "head"), [(j, i) for i, j in up])
    swap = [(i, i ^ 1) for i in range(group_count)]
    hop = [(i, i + 1) for i in range(1, group_count - 1, 2)]
    hop = hop + [(j, i) for i, j in hop]

    def tied(x, *others):
        return lax.optimization_barrier((x, *others))[0]

    one = [lax.ppermute(features, *up)]
    parcel, w_query, w_kv = prepare(features, adjacency, counts.reshape(1, NB), in_proj)
    two = [lax.ppermute(tied(features, parcel), *down)]
    from_core = lax.ppermute(parcel, "dom", swap)

    one.append(lax.ppermute(tied(one[0], w_query), *up))
    q_own, *kv_a = project([features, one[0]], gain, w_kv, w_query)
    two.append(lax.ppermute(tied(two[0], *kv_a), *down))
    from_row = lax.ppermute(tied(parcel, one[0]), "dom", hop)
    q_core, info_core = project_near(from_core, parcel, gain, w_query)
    kv_a = ((0, -1), *kv_a)
    pair = [(q_own, 0, 0), (q_core, 1, 0)]

    one.append(lax.ppermute(tied(one[1], kv_a[1]), *up))
    kv_b = project([two[0], one[1]], gain, w_kv)
    two.append(lax.ppermute(tied(two[1], *kv_b), *down))
    kv_b = ((1, -2), *kv_b)
    pair_state = attend(info_core, pair, [kv_a])
    q_cross, info = project_later(from_row, gain, w_query, tied(info_core, *pair_state))
    far = [(q_cross, 2, 0)]

    one.append(lax.ppermute(tied(one[2], kv_b[1]), *up))
    far_state = attend(info, far, [kv_a, kv_b])
    kv_c = ((2, -3), *project([two[1], one[2]], gain, w_kv))
    kv_d = ((3,), *project([two[2]], gain, w_kv))
    far_state = attend(info, far, [kv_c, kv_d], far_state)

    kv_e = ((4,), *project([tied(one[3], *far_state, *pair_state)], gain, w_kv))
    *_, to_cross = attend(info, far, [kv_e], far_state, last=True)
    cross = lax.ppermute(to_cross, "dom", hop)
    *pair_state, to_core = attend(
        info, pair, [kv_b, kv_c, kv_d, kv_e], tied(pair_state, to_cross), last=True
    )
    core = lax.ppermute(to_core, "dom", swap)
    return finish(pair_state, core, cross, out_proj, features)


def solution(mesh):
    return jax.shard_map(
        body,
        mesh=mesh,
        in_specs=(P(("dom", "head"), None), P(), P(), P(), P("dom", None), P("dom")),
        out_specs=P(("dom", "head"), None),
        check_vma=False,
    )
```
